256 devices in a mesh: row: 4 (over y), space: 64 (over z, x, core).
Axes of the slice: x: 4, y: 4, z: 8, core: 2. Of those that a mesh axis runs over, the one named last changes fastest.
Arguments:
- right_side: float32 [4, 9, 5, 32768], P('row', None, None, 'space'), may hold values from -6 to 6
- coupling: float32 [4, 6, 5, 32768], P('row', None, None, 'space'), may hold values from -0.5 to 0.5
- offsets: int32 [4, 6, 32768], P('row', None, 'space'), may hold values from -16 to 16
- block_mean: float32 [4, 5, 5, 32768], P('row', None, None, 'space'), may hold values from -0.179 to 1.51, as said below
- block_wave: float32 [4, 4, 10, 10, 32768], P('row', None, None, None, 'space'), may hold values from -0.127 to 1.51, as said below
- donor_cells: int32 [4, 1024], P('row'), may hold values from 0 to 32767
- receiver_cells: int32 [4, 1024], P('row'), may hold values from 0 to 32767
- inlet_gain: float32 [4, 5, 1024], P('row'), may hold values from 0.5 to 2
Outputs:
- solution: float32 [4, 9, 5, 32768], P('row', None, None, 'space')
The draws below stay inside these ranges and needn't reach their ends.
Inputs may be any that keep to these rules, and one draw needn't show every extreme that they name: `block_mean`: each block has a diagonal in 0.5 .. 1.5 and smaller entries off it. `block_wave`: each block has a diagonal in 0.5 .. 1.5 and smaller entries off it.
All inputs are finite; a program needn't handle non-finite values.
Results may differ from the reference program's by a relative error of at most 0.0001.
Values sent between devices are 32-bit elements; how exact they have to be, the bound alone decides.
A program may use at most 128 MiB of HBM per device.

```python
import math
import jax
import jax.numpy as jnp
from jax import lax

NI = 9
NV = 5
NOFF = 6
HALO = 16
SWEEPS = 2
NIF = 1024
ROWS = 4
CELLS = 32768


def dominant_blocks(key, dims_of, order, diag_low, diag_high):
    key_off, key_diag = jax.random.split(key)
    bound = 0.4 / math.sqrt(order)
    off_diag = jax.random.uniform(key_off, dims_of, jnp.float32, -bound, bound)
    diagonal = jnp.exp(jax.random.uniform(key_diag, dims_of, jnp.float32, math.log(diag_low), math.log(diag_high)))
    last = len(dims_of)
    identity = (lax.broadcasted_iota(jnp.int32, dims_of, last - 3) == lax.broadcasted_iota(jnp.int32, dims_of, last - 2)).astype(jnp.float32)
    return identity * diagonal + (1.0 - identity) * off_diag


def draw_block_mean(key, part):
    key = jax.random.fold_in(key, 11)
    return dominant_blocks(key, (ROWS, NV, NV, CELLS), NV, 0.5, 1.5)


def draw_block_wave(key, part):
    key = jax.random.fold_in(key, 12)
    return dominant_blocks(key, (ROWS, (NI - 1) // 2, 2 * NV, 2 * NV, CELLS), 2 * NV, 0.5, 1.5)


def plant(values, own_key, smallest, top_value):
    index_at = [jax.random.randint(jax.random.fold_in(own_key, axis), (), 0, length) for axis, length in enumerate(values.shape)]
    widest = values.shape.index(max(values.shape))
    beside = index_at[:widest] + [(index_at[widest] + 1) % values.shape[widest]] + index_at[widest + 1:]
    return values.at[tuple(index_at)].set(smallest).at[tuple(beside)].set(top_value)


def block_scale(rng, dims, cuts, least, top_value):
    level, own = 1.0, jax.random.fold_in(rng, 6)
    for dim, parts in cuts:
        draws = jnp.exp(jax.random.uniform(jax.random.fold_in(own, dim), (parts,), jnp.float32, least / len(cuts), top_value / len(cuts)))
        level = level * jnp.repeat(draws, dims[dim] // parts).reshape([-1 if axis == dim else 1 for axis in range(len(dims))])
    return level


def noise(stream_key, dims, width, reach, cuts=(), kind=jnp.bfloat16):
    drawn = jax.random.normal(stream_key, dims, jnp.float32) * width
    if len(cuts) > 0:
        drawn = block_scale(stream_key, dims, cuts, -0.22, 0.18) * drawn
    return jnp.clip(drawn, min=-reach, max=reach).astype(kind)


def setup_inputs(seed: int = 0) -> dict:
    keys = jax.random.split(jax.random.key(seed), 9)
    right_side = noise(keys[0], (ROWS, NI, NV, CELLS), 1.0, 6.0, ((0, 4), (3, 64)), jnp.float32)
    coupling = noise(keys[1], (ROWS, NOFF, NV, CELLS), 0.1, 0.5, ((0, 4), (3, 64)), jnp.float32)
    offsets = plant(jax.random.randint(keys[2], (ROWS, NOFF, CELLS), 0 - HALO, HALO + 1), jax.random.fold_in(keys[2], 1), 0 - HALO, HALO).astype(jnp.int32)
    block_mean = draw_block_mean(jax.random.fold_in(keys[8], 71), 0)
    block_wave = draw_block_wave(jax.random.fold_in(keys[8], 71), 0)
    donor_cells = plant(jax.random.randint(keys[5], (ROWS, NIF), 0, CELLS), jax.random.fold_in(keys[5], 1), 0, CELLS - 1).astype(jnp.int32)
    receiver_cells = plant(jax.random.randint(keys[6], (ROWS, NIF), 0, CELLS), jax.random.fold_in(keys[6], 1), 0, CELLS - 1).astype(jnp.int32)
    inlet_gain = jnp.clip(jnp.exp(math.log(2.0) - 1.3862944 * jax.random.uniform(keys[7], (ROWS, NV, NIF), jnp.float32) ** block_scale(keys[7], (ROWS, NV, NIF), ((0, 4),), -0.2, 0.2)), 0.5, 2.0)
    return {"right_side": right_side, "coupling": coupling, "offsets": offsets, "block_mean": block_mean, "block_wave": block_wave, "donor_cells": donor_cells, "receiver_cells": receiver_cells, "inlet_gain": inlet_gain}


def spectral_table(instances):
    position = jnp.arange(instances).astype(jnp.float32)
    harmonic = jnp.arange(1, (instances - 1) // 2 + 1).astype(jnp.float32)
    phase_angle = 2.0 * math.pi / instances * harmonic[:, None] * position[None, :]
    weight = math.sqrt(2.0 / instances)
    wave_rows = jnp.stack([weight * jnp.cos(phase_angle), weight * jnp.sin(phase_angle)], axis=1).reshape(-1, instances)
    mean_row = jnp.full((1, instances), 1.0 / math.sqrt(instances), jnp.float32)
    return jnp.concatenate([mean_row, wave_rows], axis=0)

def invert_blocks(values, block_mean, block_wave, spectral):
    spectral_modes = jnp.einsum('kn,nvc->kvc', spectral, values, precision=lax.Precision.HIGHEST)
    variables = spectral_modes.shape[1]
    harmonics = (spectral_modes.shape[0] - 1) // 2
    steady = lax.optimization_barrier(jnp.sum(block_mean * spectral_modes[0][None, :, :], axis=1))
    paired = spectral_modes[1:].reshape(harmonics, 2 * variables, spectral_modes.shape[2])
    paired = lax.optimization_barrier(jnp.sum(block_wave * paired[:, None, :, :], axis=2))
    joined = jnp.concatenate([steady[None], paired.reshape(2 * harmonics, variables, spectral_modes.shape[2])], axis=0)
    return jnp.einsum('kn,kvc->nvc', spectral, joined, precision=lax.Precision.HIGHEST)

def neighbor_sum(padded, offsets, coupling, reach_cells):
    cell_count = offsets.shape[1]
    cell_base = jnp.arange(cell_count, dtype=jnp.int32) + reach_cells
    accumulated = jnp.zeros((padded.shape[0], padded.shape[1], cell_count), jnp.float32)
    for neighbor in range(offsets.shape[0]):
        neighbor_vals = jnp.take(padded, (cell_base + offsets[neighbor]).astype(jnp.int32), axis=2)
        accumulated = accumulated + coupling[neighbor][None, :, :] * neighbor_vals
    return accumulated

def reference(right_side, coupling, offsets, block_mean, block_wave, donor_cells, receiver_cells, inlet_gain):
    spectral = spectral_table(NI)
    profile = jnp.zeros((NI, NV, NIF), jnp.float32)
    solutions = []
    for row_index in range(ROWS):
        mean_blocks = block_mean[row_index]
        wave_blocks = block_wave[row_index]
        inflow = inlet_gain[row_index][None, :, :] * profile
        source = right_side[row_index] - jnp.zeros_like(right_side[row_index]).at[:, :, receiver_cells[row_index]].add(inflow)
        state_field = invert_blocks(source, mean_blocks, wave_blocks, spectral)
        for sweep_index in range(SWEEPS):
            padded = jnp.pad(state_field, ((0, 0), (0, 0), (HALO, HALO)))
            coupled = neighbor_sum(padded, offsets[row_index], coupling[row_index], HALO)
            state_field = invert_blocks(source - coupled, mean_blocks, wave_blocks, spectral)
        solutions.append(state_field)
        profile = jnp.take(state_field, donor_cells[row_index], axis=2)
    return jnp.stack(solutions)
```

```python
import functools
import math

import jax
import jax.numpy as jnp
import numpy as np
from jax import lax
from jax.experimental import pallas as pl
from jax.experimental.pallas import tpu as pltpu
from jax.sharding import PartitionSpec as P

NI = 9
NV = 5
NF = NI * NV
NOFF = 6
HALO = 16
SWEEPS = 2
NIF = 1024
ROWS = 4
NS = 64
OWN = 512
EDGE = 32
CAP = 8
MESH = pl.DeviceIdType.MESH

HALO_ROWS = 152
AT_SIX = 144
AT_FIVE = 104
AT_TAIL = 80


def spectral_numbers():
    n = np.arange(NI, dtype=np.float64)
    table = [np.full(NI, 1.0 / math.sqrt(NI))]
    for k in range(1, (NI - 1) // 2 + 1):
        table.append(math.sqrt(2.0 / NI) * np.cos(2.0 * math.pi * k * n / NI))
        table.append(math.sqrt(2.0 / NI) * np.sin(2.0 * math.pi * k * n / NI))
    return np.stack(table).astype(np.float32)


def kernel(
    rhs_h, cpl_h, off_h, bm_h, bw_h, don_h, rec_h, gain_h,
    out_ref, flag_ref,
    rhs_v, cpl_v, off_v, bm_v, bw_v, gain_v, idx_v,
    wave_w, five_w, six_w, lane_w, src_w, x_w, y_w,
    send_left, send_right, from_left, from_right,
    code_s, sel_s, xr_s, wr_s, gpk_s, msg_s, got_s,
    in_sem, idx_send, idx_recv, edge_send, edge_recv, msg_send, msg_recv,
):
    r = lax.axis_index("row")
    s = lax.axis_index("space")

    loads = [
        pltpu.make_async_copy(bw_h.at[0], bw_v, in_sem.at[0]),
        pltpu.make_async_copy(bm_h.at[0], bm_v, in_sem.at[1]),
        pltpu.make_async_copy(cpl_h.at[0], cpl_v, in_sem.at[2]),
        pltpu.make_async_copy(rhs_h.at[0], rhs_v, in_sem.at[3]),
        pltpu.make_async_copy(off_h.at[0], off_v, in_sem.at[4]),
        pltpu.make_async_copy(gain_h.at[0], gain_v, in_sem.at[5]),
        pltpu.make_async_copy(don_h, idx_v.at[r, 0], in_sem.at[6]),
        pltpu.make_async_copy(rec_h, idx_v.at[r, 1], in_sem.at[7]),
    ]
    for c in loads:
        c.start()

    bar = pltpu.get_barrier_semaphore()

    def greet(row, t):
        pl.semaphore_signal(bar, inc=1, device_id=(row, t), device_id_type=MESH)

    @pl.when(s > 0)
    def _():
        greet(r, s - 1)

    @pl.when(s < NS - 1)
    def _():
        greet(r, s + 1)

    for row in range(ROWS):
        @pl.when((row > r + 1) | (row < r - 1))
        def _():
            greet(row, s)

    @pl.when(r < ROWS - 1)
    def _():
        def one(t, c):
            greet(r + 1, t)
            return c
        lax.fori_loop(0, NS, one, 0, unroll=8)

    @pl.when(r > 0)
    def _():
        def one(t, c):
            greet(r - 1, t)
            return c
        lax.fori_loop(0, NS, one, 0, unroll=8)

    lane8 = lax.broadcasted_iota(jnp.int32, (8, 128), 1)

    def to_windows(tiles, dst, row):
        n = tiles[0].shape[0]
        lane = lane8[:n]
        up = [pltpu.roll(t, 32, 1) for t in tiles]
        down = [pltpu.roll(t, 96, 1) for t in tiles]
        for m in range(4):
            even = up[m] if m == 0 else jnp.where(lane < 32, up[m - 1], up[m])
            odd = down[m] if m == 3 else jnp.where(lane < 96, down[m], down[m + 1])
            dst[pl.ds(row + 2 * m, n, stride=8), :] = even
            dst[pl.ds(row + 2 * m + 1, n, stride=8), :] = odd

    def pack(firsts, lasts, row):
        n = firsts[0].shape[0]
        lane = lane8[:n]
        left = firsts[0]
        right = pltpu.roll(lasts[0], 32, 1)
        for e in range(1, len(firsts)):
            left = jnp.where(lane >= 32 * e, pltpu.roll(firsts[e], 32 * e, 1), left)
            moved = lasts[e] if e == 3 else pltpu.roll(lasts[e], (32 * e + 32) % 128, 1)
            right = jnp.where(lane >= 32 * e, moved, right)
        send_left[pl.ds(row, n), :] = left
        send_right[pl.ds(row, n), :] = right

    def read_tiles(ref, lead, rows):
        return [ref[(*lead, pl.ds(rows[0], rows[1]), pl.ds(128 * m, 128))] for m in range(4)]

    loads[0].wait()

    def wave_rows(f, c):
        for g0, n, row in ((0, 8, f * 8), (8, 2, AT_TAIL + f * 2)):
            firsts, lasts = [], []
            for k in range(4):
                tiles = read_tiles(bw_v, (k, f), (g0, n))
                to_windows(tiles, wave_w, ((k * 10 + f) * 10 + g0) * 8)
                firsts.append(tiles[0])
                lasts.append(tiles[3])
            pack(firsts, lasts, row)
        return c

    lax.fori_loop(0, 10, wave_rows, 0)

    for c in loads[1:5]:
        c.wait()
    fives = [(bm_v, i) for i in range(5)] + [(cpl_v, j) for j in range(6)] + [(rhs_v, n) for n in range(9)]
    for p in range(5):
        firsts, lasts = [], []
        for e in range(4):
            ref, i = fives[4 * p + e]
            tiles = read_tiles(ref, (i,), (0, 5))
            to_windows(tiles, five_w, (4 * p + e) * 40)
            firsts.append(tiles[0])
            lasts.append(tiles[3])
        pack(firsts, lasts, AT_FIVE + 8 * p)
    tiles = [off_v[:, pl.ds(128 * m, 128)].astype(jnp.float32) for m in range(4)]
    to_windows(tiles, six_w, 0)
    pack([tiles[0]], [tiles[3]], AT_SIX)
    send_left[pl.ds(100, 4), :] = jnp.zeros((4, 128), jnp.float32)
    send_right[pl.ds(100, 4), :] = jnp.zeros((4, 128), jnp.float32)
    for p in range(5):
        send_left[pl.ds(AT_FIVE + 8 * p + 5, 3), :] = jnp.zeros((3, 128), jnp.float32)
        send_right[pl.ds(AT_FIVE + 8 * p + 5, 3), :] = jnp.zeros((3, 128), jnp.float32)
    send_left[pl.ds(AT_SIX + 6, 2), :] = jnp.zeros((2, 128), jnp.float32)
    send_right[pl.ds(AT_SIX + 6, 2), :] = jnp.zeros((2, 128), jnp.float32)
    for c in loads[5:]:
        c.wait()
    xr_s[...] = jnp.zeros(xr_s.shape, jnp.bfloat16)
    src_w[pl.ds(NF * 8, 24), :] = jnp.zeros((24, 128), jnp.float32)
    x_w[pl.ds(NF * 8, 24), :] = jnp.zeros((24, 128), jnp.float32)

    @pl.when(s == 0)
    def _():
        from_left[...] = jnp.zeros(from_left.shape, jnp.float32)

    @pl.when(s == NS - 1)
    def _():
        from_right[...] = jnp.zeros(from_right.shape, jnp.float32)

    def one_if(condition):
        return jnp.where(condition, 1, 0)

    here = one_if(s > 0) + one_if(s < NS - 1)
    here = here + (NS - 1) * (one_if(r > 0) + one_if(r < ROWS - 1)) + ROWS - 1
    pl.semaphore_wait(bar, here)

    right = pltpu.make_async_remote_copy(
        send_right, from_left, edge_send.at[0], edge_recv.at[0],
        device_id=(r, lax.rem(s + 1, NS)), device_id_type=MESH)
    left = pltpu.make_async_remote_copy(
        send_left, from_right, edge_send.at[1], edge_recv.at[1],
        device_id=(r, lax.rem(s + NS - 1, NS)), device_id_type=MESH)

    @pl.when(s < NS - 1)
    def _():
        right.start()

    @pl.when(s > 0)
    def _():
        left.start()

    index_copies = [
        pltpu.make_async_remote_copy(
            idx_v.at[r], idx_v.at[r], idx_send.at[d], idx_recv.at[d],
            device_id=(lax.rem(r + d, ROWS), s), device_id_type=MESH)
        for d in range(1, ROWS)
    ]
    for c in index_copies:
        c.start()
    for c in index_copies:
        c.wait()

    dev64 = lax.broadcasted_iota(jnp.int32, (NS, 1), 0)
    tri = (lax.broadcasted_iota(jnp.int32, (128, 128), 0) <= lax.broadcasted_iota(jnp.int32, (128, 128), 1))
    tri = tri.astype(jnp.float32).astype(jnp.bfloat16)

    def order(mask):
        before = jnp.zeros((NS, 1), jnp.float32)
        for b in range(NIF // 128):
            m = mask[:, 128 * b:128 * b + 128]
            upto = jnp.dot(m.astype(jnp.bfloat16), tri, preferred_element_type=jnp.float32)
            code_s[:, pl.ds(128 * b, 128)] = jnp.where(m > 0.5, before + upto - 1.0, -1.0)
            before = before + jnp.sum(m, axis=1, keepdims=True)

    def pick(k, value):
        return jnp.sum(jnp.where(code_s[...] == float(k), value, 0.0), axis=1, keepdims=True)

    def in_block(cells, device):
        low = device * OWN
        return (cells >= low) & (cells < low + OWN)

    def in_windows(cells, device):
        low = device * OWN - EDGE
        return (cells >= low) & (cells < low + OWN + 2 * EDGE)

    @pl.when(r < ROWS - 1)
    def _():
        donor = idx_v[r, 0]
        receiver = idx_v[r + 1, 1]
        order((in_block(donor, s) & in_windows(receiver, dev64)).astype(jnp.float32))
        place = (donor - s * OWN + 1).astype(jnp.float32)
        cell = lax.broadcasted_iota(jnp.int32, (NS, OWN), 1).astype(jnp.float32) + 1.0
        for k in range(CAP):
            hit = (pick(k, place) == cell).astype(jnp.float32).astype(jnp.bfloat16)
            sel_s[pl.ds((k % 4) * NS, NS), pl.ds((k // 4) * OWN, OWN)] = hit

    @pl.when(r > 0)
    def _():
        donor = idx_v[r - 1, 0]
        receiver = idx_v[r, 1]
        order((in_block(donor, dev64) & in_windows(receiver, s)).astype(jnp.float32))
        place = (receiver - s * OWN + EDGE + 1).astype(jnp.float32)
        position = lax.broadcasted_iota(jnp.int32, (NS, 1024), 1)
        cell = ((position // 128) * 64 + position % 128 + 1).astype(jnp.float32)
        lane = lax.broadcasted_iota(jnp.int32, (1, 128), 1)
        field = lane % 64
        for k in range(CAP):
            hit = (pick(k, place) == cell).astype(jnp.float32).astype(jnp.bfloat16)
            wr_s[pl.ds(k * NS, NS), :] = hit
        for k in range(4):
            rows = jnp.zeros((NS, 128), jnp.float32)
            for v in range(NV):
                gain = gain_v[pl.ds(v, 1), :]
                mine = (field % NV == v) & (field < NF)
                rows = rows + jnp.where(mine & (lane < 64), pick(k, gain), 0.0)
                rows = rows + jnp.where(mine & (lane >= 64), pick(k + 4, gain), 0.0)
            gpk_s[pl.ds(k * NS, NS), :] = rows

    @pl.when(s > 0)
    def _():
        right.wait_recv()

    @pl.when(s < NS - 1)
    def _():
        left.wait_recv()

    def merge(dst, row, n, src_row, e):
        lane = lane8[:n]
        low = from_left[pl.ds(src_row, n), :]
        low = low if e == 0 else pltpu.roll(low, 128 - 32 * e, 1)
        high = from_right[pl.ds(src_row, n), :]
        high = high if e == 3 else pltpu.roll(high, 96 - 32 * e, 1)
        at = pl.ds(row, n, stride=8)
        dst[at, :] = jnp.where(lane < 32, low, dst[at, :])
        at = pl.ds(row + 7, n, stride=8)
        dst[at, :] = jnp.where(lane >= 96, high, dst[at, :])

    def wave_edges(f, c):
        for k in range(4):
            merge(wave_w, (k * 10 + f) * 80, 8, f * 8, k)
            merge(wave_w, (k * 10 + f) * 80 + 64, 2, AT_TAIL + f * 2, k)
        return c

    lax.fori_loop(0, 10, wave_edges, 0)
    for p in range(5):
        for e in range(4):
            merge(five_w, (4 * p + e) * 40, 5, AT_FIVE + 8 * p, e)
    merge(six_w, 0, 6, AT_SIX, 0)

    for j in range(NOFF):
        at = lane8 + six_w[pl.ds(8 * j, 8), :].astype(jnp.int32)
        lane_w[j] = jnp.clip(at, 0, 127)

    table = spectral_numbers()
    for v in range(NV):
        parts = [five_w[pl.ds((55 + n * NV + v) * 8, 8), :] for n in range(NI)]
        for m in range(NI):
            total = float(table[m, 0]) * parts[0]
            for n in range(1, NI):
                total = total + float(table[m, n]) * parts[n]
            src_w[pl.ds((m * NV + v) * 8, 8), :] = total

    @pl.when(r > 0)
    def _():
        pltpu.make_async_remote_copy(
            msg_s, got_s, msg_send, msg_recv, device_id=(r - 1, s), device_id_type=MESH).wait_recv()
        rows = jnp.concatenate([got_s[:, k, :] for k in range(4)], axis=0) * gpk_s[...]
        turned = jnp.concatenate([rows[:128].T, rows[128:].T], axis=1)
        both = jnp.concatenate([turned[:48], turned[64:112]], axis=1)
        high = both.astype(jnp.bfloat16)
        low = (both - high.astype(jnp.float32)).astype(jnp.bfloat16)
        inflow = jnp.dot(jnp.concatenate([high, low], axis=0), wr_s[...], preferred_element_type=jnp.float32)
        inflow = inflow[:48] + inflow[48:]
        for a in range(6):
            for j in range(8):
                at = pl.ds(a * 64 + j, 8, stride=8)
                src_w[at, :] = src_w[at, :] - inflow[8 * a:8 * a + 8, 128 * j:128 * j + 128]

    def relax(first, count, block, stride):
        source = [src_w[pl.ds((first + f) * 8, 8), :] for f in range(count)]

        def solve(values):
            result = []
            for f in range(count):
                total = None
                for g in range(count):
                    term = block[pl.ds(stride + (f * count + g) * 8, 8), :] * values[g]
                    total = term if total is None else total + term
                result.append(total)
            return result

        x = solve(source)
        for _ in range(SWEEPS):
            rest = []
            for f in range(count):
                total = source[f]
                for j in range(NOFF):
                    moved = jnp.take_along_axis(x[f], lane_w[j], axis=1, mode="promise_in_bounds")
                    total = total - five_w[pl.ds((25 + j * NV + f % NV) * 8, 8), :] * moved
                rest.append(total)
            x = solve(rest)
        for f in range(count):
            x_w[pl.ds((first + f) * 8, 8), :] = x[f]

    relax(0, NV, five_w, 0)

    def harmonic(k, c):
        relax(NV + 10 * k, 10, wave_w, k * 800)
        return c

    lax.fori_loop(0, 4, harmonic, 0)

    def own_tile(ref, row, n, m):
        lane = lane8[:n]
        even = ref[pl.ds(row + 2 * m, n, stride=8), :]
        odd = ref[pl.ds(row + 2 * m + 1, n, stride=8), :]
        return jnp.where(lane < 64, pltpu.roll(even, 96, 1), pltpu.roll(odd, 32, 1))

    @pl.when(r < ROWS - 1)
    def _():
        for a in range(3):
            for m in range(4):
                tile = jnp.concatenate([own_tile(x_w, (2 * a + i) * 64, 8, m) for i in range(2)], axis=0)
                high = tile.astype(jnp.bfloat16)
                low = (tile - high.astype(jnp.float32)).astype(jnp.bfloat16)
                for half in range(2):
                    at = pl.ds(half * OWN + 128 * m, 128)
                    xr_s[pl.ds(64 * half + 16 * a, 16), at] = high
                    xr_s[pl.ds(128 + 64 * half + 16 * a, 16), at] = low
        values = lax.dot_general(
            sel_s[...], xr_s[...], (((1,), (1,)), ((), ())), preferred_element_type=jnp.float32)
        values = values[:, :128] + values[:, 128:]
        for k in range(4):
            msg_s[:, k, :] = values[k * NS:(k + 1) * NS]

        def send(j, c):
            t = lax.rem(s + j, NS)
            pltpu.make_async_remote_copy(
                msg_s.at[t], got_s.at[s], msg_send, msg_recv,
                device_id=(r + 1, t), device_id_type=MESH).start()
            return c

        lax.fori_loop(0, NS, send, 0, unroll=8)

    for v in range(NV):
        parts = [x_w[pl.ds((m * NV + v) * 8, 8), :] for m in range(NI)]
        for n in range(NI):
            total = float(table[0, n]) * parts[0]
            for m in range(1, NI):
                total = total + float(table[m, n]) * parts[m]
            y_w[pl.ds((n * NV + v) * 8, 8), :] = total
    for n in range(NI):
        for m in range(4):
            out_ref[0, n, :, pl.ds(128 * m, 128)] = own_tile(y_w, n * 40, 5, m)

    most = jnp.zeros((NS, NS), jnp.float32)
    for row in range(ROWS - 1):
        gives = in_block(idx_v[row, 0], dev64).astype(jnp.float32).astype(jnp.bfloat16)
        takes = in_windows(idx_v[row + 1, 1], dev64).astype(jnp.float32).astype(jnp.bfloat16)
        count = lax.dot_general(gives, takes, (((1,), (1,)), ((), ())), preferred_element_type=jnp.float32)
        most = jnp.maximum(most, count)
    flag_ref[...] = jnp.broadcast_to((jnp.max(most, keepdims=True) > CAP + 0.5).astype(jnp.int32), (8, 128))

    @pl.when(s < NS - 1)
    def _():
        right.wait_send()

    @pl.when(s > 0)
    def _():
        left.wait_send()

    @pl.when(r < ROWS - 1)
    def _():
        pltpu.make_async_remote_copy(
            msg_s, got_s, msg_send, msg_recv, device_id=(r + 1, s), device_id_type=MESH).wait_send()


def fast(*args):
    any_space = pl.BlockSpec(memory_space=pl.ANY)
    vmem = pl.BlockSpec(memory_space=pltpu.VMEM)
    f32, i32, bf16 = jnp.float32, jnp.int32, jnp.bfloat16
    return pl.pallas_call(
        kernel,
        out_shape=(jax.ShapeDtypeStruct((1, NI, NV, OWN), f32), jax.ShapeDtypeStruct((8, 128), i32)),
        in_specs=[any_space] * 8,
        out_specs=(vmem, vmem),
        scratch_shapes=[
            pltpu.VMEM((NI, NV, OWN), f32),
            pltpu.VMEM((NOFF, NV, OWN), f32),
            pltpu.VMEM((NOFF, OWN), i32),
            pltpu.VMEM((NV, NV, OWN), f32),
            pltpu.VMEM((4, 10, 10, OWN), f32),
            pltpu.VMEM((NV, NIF), f32),
            pltpu.VMEM((ROWS, 2, 1, NIF), i32),
            pltpu.VMEM((3200, 128), f32),
            pltpu.VMEM((800, 128), f32),
            pltpu.VMEM((48, 128), f32),
            pltpu.VMEM((NOFF, 8, 128), i32),
            pltpu.VMEM((384, 128), f32),
            pltpu.VMEM((384, 128), f32),
            pltpu.VMEM((384, 128), f32),
            pltpu.VMEM((HALO_ROWS, 128), f32),
            pltpu.VMEM((HALO_ROWS, 128), f32),
            pltpu.VMEM((HALO_ROWS, 128), f32),
            pltpu.VMEM((HALO_ROWS, 128), f32),
            pltpu.VMEM((NS, NIF), f32),
            pltpu.VMEM((4 * NS, 2 * OWN), bf16),
            pltpu.VMEM((256, 2 * OWN), bf16),
            pltpu.VMEM((CAP * NS, 1024), bf16),
            pltpu.VMEM((4 * NS, 128), f32),
            pltpu.VMEM((NS, 4, 128), f32),
            pltpu.VMEM((NS, 4, 128), f32),
            pltpu.SemaphoreType.DMA((8,)),
            pltpu.SemaphoreType.DMA((ROWS,)),
            pltpu.SemaphoreType.DMA((ROWS,)),
            pltpu.SemaphoreType.DMA((2,)),
            pltpu.SemaphoreType.DMA((2,)),
            pltpu.SemaphoreType.DMA,
            pltpu.SemaphoreType.DMA,
        ],
        compiler_params=pltpu.CompilerParams(
            collective_id=0, has_side_effects=True, vmem_limit_bytes=40 * 1024 * 1024),
    )(*args)


def with_halo(block, sides, width):
    for axis, dim in sides:
        count = lax.axis_size(axis)
        forward = [(i, i + 1) for i in range(count - 1)]
        backward = [(target, source) for source, target in forward]
        low = lax.ppermute(
            lax.slice_in_dim(block, block.shape[dim] - width, None, axis=dim), axis, forward
        )
        high = lax.ppermute(lax.slice_in_dim(block, 0, width, axis=dim), axis, backward)
        block = jnp.concatenate([low, block, high], axis=dim)
    return block


def from_behind(value, axis, steps):
    count = lax.axis_size(axis)
    first, last = (max(0, -steps), min(count, count - steps))
    return lax.ppermute(value, axis, [(source, source + steps) for source in range(first, last)])


def spectral_table(instances):
    position = jnp.arange(instances).astype(jnp.float32)
    harmonic = jnp.arange(1, (instances - 1) // 2 + 1).astype(jnp.float32)
    phase_angle = 2.0 * math.pi / instances * harmonic[:, None] * position[None, :]
    weight = math.sqrt(2.0 / instances)
    wave_rows = jnp.stack(
        [weight * jnp.cos(phase_angle), weight * jnp.sin(phase_angle)], axis=1
    ).reshape(-1, instances)
    mean_row = jnp.full((1, instances), 1.0 / math.sqrt(instances), jnp.float32)
    return jnp.concatenate([mean_row, wave_rows], axis=0)


def invert_blocks(values, block_mean, block_wave, spectral):
    spectral_modes = jnp.einsum("kn,nvc->kvc", spectral, values, precision=lax.Precision.HIGHEST)
    variables = spectral_modes.shape[1]
    harmonics = (spectral_modes.shape[0] - 1) // 2
    steady = jnp.sum(block_mean * spectral_modes[0][None, :, :], axis=1)
    paired = spectral_modes[1:].reshape(harmonics, 2 * variables, spectral_modes.shape[2])
    paired = jnp.sum(block_wave * paired[:, None, :, :], axis=2)
    joined = jnp.concatenate(
        [steady[None], paired.reshape(2 * harmonics, variables, spectral_modes.shape[2])], axis=0
    )
    return jnp.einsum("kn,kvc->nvc", spectral, joined, precision=lax.Precision.HIGHEST)


def neighbor_sum(padded, offsets, coupling, reach_cells):
    cell_count = offsets.shape[1]
    cell_base = jnp.arange(cell_count, dtype=jnp.int32) + reach_cells
    accumulated = jnp.zeros((padded.shape[0], padded.shape[1], cell_count), jnp.float32)
    for neighbor in range(offsets.shape[0]):
        neighbor_vals = jnp.take(padded, cell_base + offsets[neighbor], axis=2)
        accumulated = accumulated + coupling[neighbor][None, :, :] * neighbor_vals
    return accumulated


def general(
    right_side, coupling, offsets, block_mean, block_wave, donor_cells, receiver_cells, inlet_gain
):
    space_rank = lax.axis_index("space")
    source_base = right_side[0]
    cell_count = source_base.shape[2]
    spectral = spectral_table(source_base.shape[0])
    first_cell = space_rank * cell_count
    mean_blocks = block_mean[0]
    wave_blocks = block_wave[0]

    def apply_inverse(values):
        return invert_blocks(values, mean_blocks, wave_blocks, spectral)

    donor_local = donor_cells[0] - first_cell
    donor_inside = ((donor_local >= 0) & (donor_local < cell_count)).astype(jnp.float32)
    donor_clip = jnp.clip(donor_local, 0, cell_count - 1)
    receiver_local = receiver_cells[0] - first_cell
    receiver_inside = ((receiver_local >= 0) & (receiver_local < cell_count)).astype(jnp.float32)
    receiver_clip = jnp.clip(receiver_local, 0, cell_count - 1)
    row_total = lax.axis_size("row")
    inlet_profile = jnp.zeros((NI, NV, NIF), jnp.float32)
    state_field = source_base
    for row_step in range(row_total):
        inflow = inlet_gain[0][None, :, :] * inlet_profile * receiver_inside[None, None, :]
        source = source_base - jnp.zeros_like(source_base).at[:, :, receiver_clip].add(inflow)
        state_field = apply_inverse(source)
        for sweep_index in range(SWEEPS):
            padded = with_halo(state_field, (("space", 2),), HALO)
            coupled = neighbor_sum(padded, offsets[0], coupling[0], HALO)
            state_field = apply_inverse(source - coupled)
        if row_step + 1 < row_total:
            outgoing = jnp.take(state_field, donor_clip, axis=2) * donor_inside[None, None, :]
            summed = lax.psum(outgoing, "space")
            arrived = from_behind(summed, "row", 1)
            inlet_profile = arrived
    return state_field[None]


def on_device(*args):
    result, flag = fast(*args)
    return lax.cond(flag[0, 0] > 0, lambda: general(*args), lambda: result)


def solution(mesh):
    return jax.shard_map(
        on_device,
        mesh=mesh,
        in_specs=(
            P("row", None, None, "space"),
            P("row", None, None, "space"),
            P("row", None, "space"),
            P("row", None, None, "space"),
            P("row", None, None, None, "space"),
            P("row", None),
            P("row", None),
            P("row", None, None),
        ),
        out_specs=P("row", None, None, "space"),
        check_vma=False,
    )
```

```python
import functools
import math

import jax
import jax.numpy as jnp
import numpy as np
from jax import lax
from jax.experimental import pallas as pl
from jax.experimental.pallas import tpu as pltpu
from jax.sharding import PartitionSpec as P

NI = 9
NV = 5
NF = NI * NV
NOFF = 6
HALO = 16
SWEEPS = 2
NIF = 1024
ROWS = 4
NS = 64
GROUP = 8
OWN = 512
EDGE = 32
CAP = 8
MESH = pl.DeviceIdType.MESH

HALO_ROWS = 136
AT_BASE = 104
BASE = ((0, 25), (25, 30), (55, 45), (100, 6))


def field_row(f):
    return (f if f < 25 else f + 7) * 8


def spectral_numbers():
    n = np.arange(NI, dtype=np.float64)
    table = [np.full(NI, 1.0 / math.sqrt(NI))]
    for k in range(1, (NI - 1) // 2 + 1):
        table.append(math.sqrt(2.0 / NI) * np.cos(2.0 * math.pi * k * n / NI))
        table.append(math.sqrt(2.0 / NI) * np.sin(2.0 * math.pi * k * n / NI))
    return np.stack(table).astype(np.float32)


def kernel(
    rhs_h, cpl_h, off_h, bm_h, bw_h, don_h, rec_h, gain_h,
    out_ref, flag_ref,
    rhs_v, cpl_v, off_v, bm_v, bw_v, gain_v, idx_v,
    wave_w, base_w, edge_s, lane_w, src_w, x_w, y_w,
    send_left, send_right, from_left, from_right,
    code_s, sel_s, xr_s, wr_s, gpk_s, msg_s, got_s,
    in_sem, idx_send, idx_recv, edge_send, edge_recv, msg_send, msg_recv, ready,
):
    r = lax.axis_index("row")
    s = lax.axis_index("space")

    z, p = s // GROUP, s % GROUP

    bar = pltpu.get_barrier_semaphore()

    def greet(row, t):
        pl.semaphore_signal(bar, inc=1, device_id=(row, t), device_id_type=MESH)

    @pl.when(r < ROWS - 1)
    def _():
        for j in range(GROUP):
            greet(r + 1, j * GROUP + p)

    @pl.when(r > 0)
    def _():
        for j in range(GROUP):
            greet(r - 1, j * GROUP + p)

    for j in range(1, GROUP):
        greet(r, z * GROUP + lax.rem(p + j, GROUP))

    @pl.when((p == 0) & (s > 0))
    def _():
        greet(r, s - 1)

    @pl.when((p == GROUP - 1) & (s < NS - 1))
    def _():
        greet(r, s + 1)

    for row in range(ROWS):
        @pl.when((row > r + 1) | (row < r - 1))
        def _():
            greet(row, s)

    loads = [
        pltpu.make_async_copy(bw_h, bw_v, in_sem.at[0]),
        pltpu.make_async_copy(bm_h, bm_v, in_sem.at[1]),
        pltpu.make_async_copy(cpl_h, cpl_v, in_sem.at[2]),
        pltpu.make_async_copy(rhs_h, rhs_v, in_sem.at[3]),
        pltpu.make_async_copy(off_h, off_v, in_sem.at[4]),
        pltpu.make_async_copy(gain_h, gain_v, in_sem.at[5]),
        pltpu.make_async_copy(don_h, idx_v.at[r, 0], in_sem.at[6]),
        pltpu.make_async_copy(rec_h, idx_v.at[r, 1], in_sem.at[7]),
    ]
    for c in loads:
        c.start()

    lane8 = lax.broadcasted_iota(jnp.int32, (8, 128), 1)

    def to_windows(tiles, dst, row):
        n = tiles[0].shape[0]
        lane = lane8[:n]
        up = [pltpu.roll(t, 32, 1) for t in tiles]
        down = [pltpu.roll(t, 96, 1) for t in tiles]
        for m in range(4):
            even = up[m] if m == 0 else jnp.where(lane < 32, up[m - 1], up[m])
            odd = down[m] if m == 3 else jnp.where(lane < 96, down[m], down[m + 1])
            dst[pl.ds(row + 2 * m, n, stride=8), :] = even
            dst[pl.ds(row + 2 * m + 1, n, stride=8), :] = odd

    def pack(firsts, lasts, row):
        n = firsts[0].shape[0]
        lane = lane8[:n]
        left = firsts[0]
        right = pltpu.roll(lasts[0], 32, 1)
        for e in range(1, len(firsts)):
            left = jnp.where(lane >= 32 * e, pltpu.roll(firsts[e], 32 * e, 1), left)
            moved = lasts[e] if e == 3 else pltpu.roll(lasts[e], (32 * e + 32) % 128, 1)
            right = jnp.where(lane >= 32 * e, moved, right)
        send_left[pl.ds(row, n), :] = left
        send_right[pl.ds(row, n), :] = right

    loads[0].wait()

    def wave_units(first, count, row):
        firsts, lasts = [], []
        for e in range(count):
            tiles = [
                jnp.concatenate([bw_v[2 * (first + e) + i, :, pl.ds(128 * m, 128)] for i in range(2)], axis=0)
                for m in range(4)
            ]
            to_windows(tiles, wave_w, (first + e) * 64)
            firsts.append(tiles[0])
            lasts.append(tiles[3])
        pack(firsts, lasts, row)

    def wave_rows(p, c):
        wave_units(4 * p, 4, 8 * p)
        return c

    lax.fori_loop(0, 12, wave_rows, 0)
    wave_units(48, 2, 96)

    for c in loads[1:5]:
        c.wait()
    lane4 = lane8[:4]
    row4 = lax.broadcasted_iota(jnp.int32, (4, 128), 0)
    for ref, (first, count) in zip((bm_v, cpl_v, rhs_v, off_v), BASE):
        def base_rows(i, c, ref=ref, first=first):
            tile = ref[i].astype(jnp.float32)
            up = pltpu.roll(tile, 32, 1)
            down = pltpu.roll(tile, 96, 1)
            at = (first + i) * 8
            base_w[pl.ds(at, 4, stride=2), :] = jnp.where(lane4 < 32, pltpu.roll(up, 1, 0), up)
            base_w[pl.ds(at + 1, 4, stride=2), :] = jnp.where(lane4 < 96, down, pltpu.roll(down, 3, 0))
            edge_s[0, pl.ds(first + i, 1), :] = tile[0:1]
            edge_s[1, pl.ds(first + i, 1), :] = tile[3:4]
            return c
        lax.fori_loop(0, count, base_rows, 0, unroll=5 if count % 5 == 0 else 6)
    edge_s[:, pl.ds(106, 22), :] = jnp.zeros((2, 22, 128), jnp.float32)
    for q in range(4):
        pack(
            [edge_s[0, pl.ds(32 * e + 8 * q, 8), :] for e in range(4)],
            [edge_s[1, pl.ds(32 * e + 8 * q, 8), :] for e in range(4)], AT_BASE + 8 * q)
    for c in loads[5:]:
        c.wait()
    xr_s[...] = jnp.zeros(xr_s.shape, jnp.bfloat16)
    for ref in (src_w, x_w):
        ref[pl.ds(200, 56), :] = jnp.zeros((56, 128), jnp.float32)
        ref[pl.ds(416, 96), :] = jnp.zeros((96, 128), jnp.float32)

    @pl.when(s == 0)
    def _():
        from_left[...] = jnp.zeros(from_left.shape, jnp.float32)

    @pl.when(s == NS - 1)
    def _():
        from_right[...] = jnp.zeros(from_right.shape, jnp.float32)

    def one_if(condition):
        return jnp.where(condition, 1, 0)

    here = GROUP * (one_if(r > 0) + one_if(r < ROWS - 1)) + GROUP - 1
    here = here + one_if((p == 0) & (s > 0)) + one_if((p == GROUP - 1) & (s < NS - 1))
    here = here + 1 + one_if(r == 0) + one_if(r == ROWS - 1)
    pl.semaphore_wait(bar, here)

    right = pltpu.make_async_remote_copy(
        send_right, from_left, edge_send.at[0], edge_recv.at[0],
        device_id=(r, lax.rem(s + 1, NS)), device_id_type=MESH)
    left = pltpu.make_async_remote_copy(
        send_left, from_right, edge_send.at[1], edge_recv.at[1],
        device_id=(r, lax.rem(s + NS - 1, NS)), device_id_type=MESH)

    @pl.when(s < NS - 1)
    def _():
        right.start()

    @pl.when(s > 0)
    def _():
        left.start()

    index_copies = [
        pltpu.make_async_remote_copy(
            idx_v.at[r], idx_v.at[r], idx_send.at[d], idx_recv.at[d],
            device_id=(lax.rem(r + d, ROWS), s), device_id_type=MESH)
        for d in range(1, ROWS)
    ]
    for c in index_copies:
        c.start()

    @pl.when(r > 0)
    def _():
        for j in range(GROUP):
            pl.semaphore_signal(ready, inc=1, device_id=(r - 1, j * GROUP + p), device_id_type=MESH)

    dev64 = lax.broadcasted_iota(jnp.int32, (NS, 1), 0)
    tri = (lax.broadcasted_iota(jnp.int32, (128, 128), 0) <= lax.broadcasted_iota(jnp.int32, (128, 128), 1))
    tri = tri.astype(jnp.float32).astype(jnp.bfloat16)

    def order(mask):
        before = jnp.zeros((NS, 1), jnp.float32)
        for b in range(NIF // 128):
            m = mask[:, 128 * b:128 * b + 128]
            upto = jnp.dot(m.astype(jnp.bfloat16), tri, preferred_element_type=jnp.float32)
            code_s[:, pl.ds(128 * b, 128)] = jnp.where(m > 0.5, before + upto - 1.0, -1.0)
            before = before + jnp.sum(m, axis=1, keepdims=True)

    def pick(k, value):
        return jnp.sum(jnp.where(code_s[...] == float(k), value, 0.0), axis=1, keepdims=True)

    def in_block(cells, device):
        low = device * OWN
        return (cells >= low) & (cells < low + OWN)

    def in_windows(cells, device):
        low = device * OWN - EDGE
        return (cells >= low) & (cells < low + OWN + 2 * EDGE)

    @pl.when(r < ROWS - 1)
    def _():
        index_copies[2].wait_recv()
        donor = idx_v[r, 0]
        receiver = idx_v[r + 1, 1]
        order((in_block(donor, s) & in_windows(receiver, dev64)).astype(jnp.float32))
        place = (donor - s * OWN + 1).astype(jnp.float32)
        cell = lax.broadcasted_iota(jnp.int32, (NS, OWN), 1).astype(jnp.float32) + 1.0
        for k in range(CAP):
            hit = (pick(k, place) == cell).astype(jnp.float32).astype(jnp.bfloat16)
            sel_s[pl.ds(k * NS, NS), :] = hit

    @pl.when(r > 0)
    def _():
        index_copies[0].wait_recv()
        donor = idx_v[r - 1, 0]
        receiver = idx_v[r, 1]
        order((in_block(donor, dev64) & in_windows(receiver, s)).astype(jnp.float32))
        place = (receiver - s * OWN + EDGE + 1).astype(jnp.float32)
        position = lax.broadcasted_iota(jnp.int32, (NS, 1024), 1)
        cell = ((position // 128) * 64 + position % 128 + 1).astype(jnp.float32)
        lane = lax.broadcasted_iota(jnp.int32, (1, 128), 1)
        field = lane % 32
        for k in range(CAP):
            hit = (pick(k, place) == cell).astype(jnp.float32).astype(jnp.bfloat16)
            wr_s[pl.ds(k * NS, NS), :] = hit
        for k in range(2):
            rows = jnp.zeros((NS, 128), jnp.float32)
            for v in range(NV):
                for g in range(4):
                    mine = (field % NV == v) & (field < 25) & (lane // 32 == g)
                    rows = rows + jnp.where(mine, pick(2 * g + k, gain_v[v]), 0.0)
            gpk_s[pl.ds(k * NS, NS), :] = rows

    @pl.when(s > 0)
    def _():
        right.wait_recv()

    @pl.when(s < NS - 1)
    def _():
        left.wait_recv()

    def merge(dst, row, n, src_row, e):
        lane = lane8[:n]
        low = from_left[pl.ds(src_row, n), :]
        low = low if e == 0 else pltpu.roll(low, 128 - 32 * e, 1)
        high = from_right[pl.ds(src_row, n), :]
        high = high if e == 3 else pltpu.roll(high, 96 - 32 * e, 1)
        at = pl.ds(row, n, stride=8)
        dst[at, :] = jnp.where(lane < 32, low, dst[at, :])
        at = pl.ds(row + 7, n, stride=8)
        dst[at, :] = jnp.where(lane >= 96, high, dst[at, :])

    def wave_edges(p, c):
        for e in range(4):
            merge(wave_w, (4 * p + e) * 64, 8, 8 * p, e)
        return c

    lax.fori_loop(0, 12, wave_edges, 0)
    for e in range(2):
        merge(wave_w, (48 + e) * 64, 8, 96, e)
    for e in range(4):
        for q in range(4 if e < 3 else 2):
            merge(base_w, (32 * e + 8 * q) * 8, 8, AT_BASE + 8 * q, e)

    for j in range(NOFF):
        at = lane8 + base_w[pl.ds((100 + j) * 8, 8), :].astype(jnp.int32)
        lane_w[j] = jnp.clip(at, 0, 127)

    table = spectral_numbers()
    for v in range(NV):
        parts = [base_w[pl.ds((55 + n * NV + v) * 8, 8), :] for n in range(NI)]
        for m in range(NI):
            total = float(table[m, 0]) * parts[0]
            for n in range(1, NI):
                total = total + float(table[m, n]) * parts[n]
            src_w[pl.ds(field_row(m * NV + v), 8), :] = total

    def inflow(h):
        pltpu.make_async_remote_copy(
            msg_s.at[h], got_s.at[h], msg_send.at[h], msg_recv.at[h],
            device_id=(r - 1, s), device_id_type=MESH).wait_recv()
        rows = jnp.concatenate([got_s[h, :, k, :] for k in range(2)], axis=0) * gpk_s[...]
        turned = rows.T
        both = jnp.concatenate([turned[32 * g:32 * g + 32] for g in range(4)], axis=1)
        high = both.astype(jnp.bfloat16)
        low = (both - high.astype(jnp.float32)).astype(jnp.bfloat16)
        added = jnp.dot(jnp.concatenate([high, low], axis=0), wr_s[...], preferred_element_type=jnp.float32)
        added = added[:32] + added[32:]
        for a in range(4 - h):
            for j in range(8):
                at = pl.ds(h * 256 + a * 64 + j, 8, stride=8)
                src_w[at, :] = src_w[at, :] - added[8 * a:8 * a + 8, 128 * j:128 * j + 128]

    def relax(row, count, entry):
        source = [src_w[pl.ds(row + f * 8, 8), :] for f in range(count)]

        def solve(values):
            result = []
            for f in range(count):
                total = None
                for g in range(count):
                    term = entry(f, g) * values[g]
                    total = term if total is None else total + term
                result.append(total)
            return result

        x = solve(source)
        for _ in range(SWEEPS):
            rest = list(source)
            for j in range(NOFF):
                at = lane_w[j]
                for f in range(count):
                    moved = jnp.take_along_axis(x[f], at, axis=1, mode="promise_in_bounds")
                    rest[f] = rest[f] - base_w[pl.ds((25 + j * NV + f % NV) * 8, 8), :] * moved
            x = solve(rest)
        for f in range(count):
            x_w[pl.ds(row + f * 8, 8), :] = x[f]

    def harmonic(k, c):
        row = jnp.where(k < 2, 40 + 80 * k, 256 + 80 * (k - 2))
        relax(row, 10, lambda f, g: wave_w[pl.ds((f * 10 + g) * 32 + k * 8, 8), :])
        return c

    def relax_half(h):
        if h == 0:
            relax(0, NV, lambda f, g: base_w[pl.ds((f * NV + g) * 8, 8), :])
        lax.fori_loop(2 * h, 2 * h + 2, harmonic, 0)

    def own_tile(ref, row, n, m):
        lane = lane8[:n]
        even = ref[pl.ds(row + 2 * m, n, stride=8), :]
        odd = ref[pl.ds(row + 2 * m + 1, n, stride=8), :]
        return jnp.where(lane < 64, pltpu.roll(even, 96, 1), pltpu.roll(odd, 32, 1))

    def donate(h):
        for a in range(2):
            for m in range(4):
                tile = jnp.concatenate(
                    [own_tile(x_w, h * 256 + (2 * a + i) * 64, 8, m) for i in range(2)], axis=0)
                high = tile.astype(jnp.bfloat16)
                low = (tile - high.astype(jnp.float32)).astype(jnp.bfloat16)
                xr_s[pl.ds(16 * a, 16), pl.ds(128 * m, 128)] = high
                xr_s[pl.ds(128 + 16 * a, 16), pl.ds(128 * m, 128)] = low
        values = lax.dot_general(
            sel_s[...], xr_s[...], (((1,), (1,)), ((), ())), preferred_element_type=jnp.float32)
        values = values[:, :128] + values[:, 128:]
        for k in range(2):
            rows = values[k * NS:(k + 1) * NS]
            for g in range(1, 4):
                at = (2 * g + k) * NS
                rows = rows + pltpu.roll(values[at:at + NS], 32 * g, 1)
            msg_s[h, :, k, :] = rows
        if h == 0:
            pl.semaphore_wait(ready, GROUP)

        def send(j, c):
            t = lax.rem(s + 36 + j, NS)
            pltpu.make_async_remote_copy(
                msg_s.at[h, t], got_s.at[h, s], msg_send.at[h], msg_recv.at[h],
                device_id=(r + 1, t), device_id_type=MESH).start()
            return c

        lax.fori_loop(0, NS, send, 0, unroll=8)

    for h in range(2):
        @pl.when(r > 0)
        def _():
            inflow(h)

        relax_half(h)

        @pl.when(r < ROWS - 1)
        def _():
            donate(h)

    for v in range(NV):
        parts = [x_w[pl.ds(field_row(m * NV + v), 8), :] for m in range(NI)]
        for n in range(NI):
            total = float(table[0, n]) * parts[0]
            for m in range(1, NI):
                total = total + float(table[m, n]) * parts[m]
            y_w[pl.ds((n * NV + v) * 8, 8), :] = total
    def out_rows(i, c):
        even = y_w[pl.ds(i * 8, 4, stride=2), :]
        odd = y_w[pl.ds(i * 8 + 1, 4, stride=2), :]
        out_ref[i] = jnp.where(lane4 < 64, pltpu.roll(even, 96, 1), pltpu.roll(odd, 32, 1))
        return c

    lax.fori_loop(0, NF, out_rows, 0, unroll=5)

    @pl.when(r == ROWS - 1)
    def _():
        index_copies[2].wait_recv()

    @pl.when(r == 0)
    def _():
        index_copies[0].wait_recv()

    index_copies[1].wait_recv()
    for c in index_copies:
        c.wait_send()
    most = jnp.zeros((NS, NS), jnp.float32)
    for row in range(ROWS - 1):
        gives = in_block(idx_v[row, 0], dev64).astype(jnp.float32).astype(jnp.bfloat16)
        takes = in_windows(idx_v[row + 1, 1], dev64).astype(jnp.float32).astype(jnp.bfloat16)
        count = lax.dot_general(gives, takes, (((1,), (1,)), ((), ())), preferred_element_type=jnp.float32)
        most = jnp.maximum(most, count)
    flag_ref[0, 0] = jnp.where(jnp.max(most) > CAP + 0.5, 1, 0)

    @pl.when(s < NS - 1)
    def _():
        right.wait_send()

    @pl.when(s > 0)
    def _():
        left.wait_send()

    @pl.when(r < ROWS - 1)
    def _():
        for h in range(2):
            pltpu.make_async_remote_copy(
                msg_s.at[h], got_s.at[h], msg_send.at[h], msg_recv.at[h],
                device_id=(r + 1, s), device_id_type=MESH).wait_send()


def fast(rhs, cpl, off, bm, bw, don, rec, gain):
    bw = jnp.transpose(bw, (0, 2, 3, 1, 4)).reshape(100, 4, OWN)
    rhs, cpl, off, bm = (a.reshape(-1, 4, 128) for a in (rhs, cpl, off, bm))
    gain = gain.reshape(NV, 1, NIF)
    any_space = pl.BlockSpec(memory_space=pl.ANY)
    vmem = pl.BlockSpec(memory_space=pltpu.VMEM)
    f32, i32, bf16 = jnp.float32, jnp.int32, jnp.bfloat16
    return pl.pallas_call(
        kernel,
        out_shape=(jax.ShapeDtypeStruct((NF, 4, 128), f32), jax.ShapeDtypeStruct((1, 1), i32)),
        in_specs=[any_space] * 8,
        out_specs=(vmem, pl.BlockSpec(memory_space=pltpu.SMEM)),
        scratch_shapes=[
            pltpu.VMEM((NF, 4, 128), f32),
            pltpu.VMEM((NOFF * NV, 4, 128), f32),
            pltpu.VMEM((NOFF, 4, 128), i32),
            pltpu.VMEM((NV * NV, 4, 128), f32),
            pltpu.VMEM((100, 4, OWN), f32),
            pltpu.VMEM((NV, 1, NIF), f32),
            pltpu.VMEM((ROWS, 2, 1, NIF), i32),
            pltpu.VMEM((3200, 128), f32),
            pltpu.VMEM((1024, 128), f32),
            pltpu.VMEM((2, 128, 128), f32),
            pltpu.VMEM((NOFF, 8, 128), i32),
            pltpu.VMEM((512, 128), f32),
            pltpu.VMEM((512, 128), f32),
            pltpu.VMEM((384, 128), f32),
            pltpu.VMEM((HALO_ROWS, 128), f32),
            pltpu.VMEM((HALO_ROWS, 128), f32),
            pltpu.VMEM((HALO_ROWS, 128), f32),
            pltpu.VMEM((HALO_ROWS, 128), f32),
            pltpu.VMEM((NS, NIF), f32),
            pltpu.VMEM((CAP * NS, OWN), bf16),
            pltpu.VMEM((256, OWN), bf16),
            pltpu.VMEM((CAP * NS, 1024), bf16),
            pltpu.VMEM((2 * NS, 128), f32),
            pltpu.VMEM((2, NS, 2, 128), f32),
            pltpu.VMEM((2, NS, 2, 128), f32),
            pltpu.SemaphoreType.DMA((8,)),
            pltpu.SemaphoreType.DMA((ROWS,)),
            pltpu.SemaphoreType.DMA((ROWS,)),
            pltpu.SemaphoreType.DMA((2,)),
            pltpu.SemaphoreType.DMA((2,)),
            pltpu.SemaphoreType.DMA((2,)),
            pltpu.SemaphoreType.DMA((2,)),
            pltpu.SemaphoreType.REGULAR,
        ],
        compiler_params=pltpu.CompilerParams(
            collective_id=0, has_side_effects=True, vmem_limit_bytes=40 * 1024 * 1024),
    )(rhs, cpl, off, bm, bw, don, rec, gain)


def with_halo(block, sides, width):
    for axis, dim in sides:
        count = lax.axis_size(axis)
        forward = [(i, i + 1) for i in range(count - 1)]
        backward = [(target, source) for source, target in forward]
        low = lax.ppermute(
            lax.slice_in_dim(block, block.shape[dim] - width, None, axis=dim), axis, forward
        )
        high = lax.ppermute(lax.slice_in_dim(block, 0, width, axis=dim), axis, backward)
        block = jnp.concatenate([low, block, high], axis=dim)
    return block


def from_behind(value, axis, steps):
    count = lax.axis_size(axis)
    first, last = (max(0, -steps), min(count, count - steps))
    return lax.ppermute(value, axis, [(source, source + steps) for source in range(first, last)])


def sum_over(value, axis):
    count = lax.axis_size(axis)
    step = 1
    while step < count:
        value = value + lax.ppermute(value, axis, [(i, i ^ step) for i in range(count)])
        step *= 2
    return value


def spectral_table(instances):
    position = jnp.arange(instances).astype(jnp.float32)
    harmonic = jnp.arange(1, (instances - 1) // 2 + 1).astype(jnp.float32)
    phase_angle = 2.0 * math.pi / instances * harmonic[:, None] * position[None, :]
    weight = math.sqrt(2.0 / instances)
    wave_rows = jnp.stack(
        [weight * jnp.cos(phase_angle), weight * jnp.sin(phase_angle)], axis=1
    ).reshape(-1, instances)
    mean_row = jnp.full((1, instances), 1.0 / math.sqrt(instances), jnp.float32)
    return jnp.concatenate([mean_row, wave_rows], axis=0)


def invert_blocks(values, block_mean, block_wave, spectral):
    spectral_modes = jnp.einsum("kn,nvc->kvc", spectral, values, precision=lax.Precision.HIGHEST)
    variables = spectral_modes.shape[1]
    harmonics = (spectral_modes.shape[0] - 1) // 2
    steady = jnp.sum(block_mean * spectral_modes[0][None, :, :], axis=1)
    paired = spectral_modes[1:].reshape(harmonics, 2 * variables, spectral_modes.shape[2])
    paired = jnp.sum(block_wave * paired[:, None, :, :], axis=2)
    joined = jnp.concatenate(
        [steady[None], paired.reshape(2 * harmonics, variables, spectral_modes.shape[2])], axis=0
    )
    return jnp.einsum("kn,kvc->nvc", spectral, joined, precision=lax.Precision.HIGHEST)


def neighbor_sum(padded, offsets, coupling, reach_cells):
    cell_count = offsets.shape[1]
    cell_base = jnp.arange(cell_count, dtype=jnp.int32) + reach_cells
    accumulated = jnp.zeros((padded.shape[0], padded.shape[1], cell_count), jnp.float32)
    for neighbor in range(offsets.shape[0]):
        neighbor_vals = jnp.take(padded, cell_base + offsets[neighbor], axis=2)
        accumulated = accumulated + coupling[neighbor][None, :, :] * neighbor_vals
    return accumulated


def general(
    right_side, coupling, offsets, block_mean, block_wave, donor_cells, receiver_cells, inlet_gain
):
    space_rank = lax.axis_index("space")
    source_base = right_side[0]
    cell_count = source_base.shape[2]
    spectral = spectral_table(source_base.shape[0])
    first_cell = space_rank * cell_count
    mean_blocks = block_mean[0]
    wave_blocks = block_wave[0]

    def apply_inverse(values):
        return invert_blocks(values, mean_blocks, wave_blocks, spectral)

    donor_local = donor_cells[0] - first_cell
    donor_inside = ((donor_local >= 0) & (donor_local < cell_count)).astype(jnp.float32)
    donor_clip = jnp.clip(donor_local, 0, cell_count - 1)
    receiver_local = receiver_cells[0] - first_cell
    receiver_inside = ((receiver_local >= 0) & (receiver_local < cell_count)).astype(jnp.float32)
    receiver_clip = jnp.clip(receiver_local, 0, cell_count - 1)
    row_total = lax.axis_size("row")
    inlet_profile = jnp.zeros((NI, NV, NIF), jnp.float32)

    def row(_, carry):
        inlet_profile, _ = carry
        inflow = inlet_gain[0][None, :, :] * inlet_profile * receiver_inside[None, None, :]
        source = source_base - jnp.zeros_like(source_base).at[:, :, receiver_clip].add(inflow)

        def sweep(_, state):
            padded = with_halo(state, (("space", 2),), HALO)
            coupled = neighbor_sum(padded, offsets[0], coupling[0], HALO)
            return apply_inverse(source - coupled)

        state_field = lax.fori_loop(0, SWEEPS, sweep, apply_inverse(source))
        outgoing = jnp.take(state_field, donor_clip, axis=2) * donor_inside[None, None, :]
        return from_behind(sum_over(outgoing, "space"), "row", 1), state_field

    return lax.fori_loop(0, row_total, row, (inlet_profile, source_base))[1][None]


def on_device(*args):
    result, flag = fast(*args)
    return lax.cond(flag[0, 0] > 0, lambda: general(*args), lambda: jnp.where(flag[0, 0] > 1, 0.0, result).reshape(1, NI, NV, OWN))


def solution(mesh):
    return jax.shard_map(
        on_device,
        mesh=mesh,
        in_specs=(
            P("row", None, None, "space"),
            P("row", None, None, "space"),
            P("row", None, "space"),
            P("row", None, None, "space"),
            P("row", None, None, None, "space"),
            P("row", None),
            P("row", None),
            P("row", None, None),
        ),
        out_specs=P("row", None, None, "space"),
        check_vma=False,
    )
```

```python
import functools
import math

import jax
import jax.numpy as jnp
import numpy as np
from jax import lax
from jax.experimental import pallas as pl
from jax.experimental.pallas import tpu as pltpu
from jax.sharding import PartitionSpec as P

NI = 9
NV = 5
NF = NI * NV
NOFF = 6
HALO = 16
SWEEPS = 2
NIF = 1024
ROWS = 4
NS = 64
GROUP = 8
OWN = 512
EDGE = 32
CAP = 8
MESH = pl.DeviceIdType.MESH

HALO_ROWS = 136
AT_BASE = 104
AT_SOURCE = 512


def field_row(f):
    return (f if f < 25 else f + 7) * 8


def spectral_numbers():
    n = np.arange(NI, dtype=np.float64)
    table = [np.full(NI, 1.0 / math.sqrt(NI))]
    for k in range(1, (NI - 1) // 2 + 1):
        table.append(math.sqrt(2.0 / NI) * np.cos(2.0 * math.pi * k * n / NI))
        table.append(math.sqrt(2.0 / NI) * np.sin(2.0 * math.pi * k * n / NI))
    return np.stack(table).astype(np.float32)


def own_tile(ref, row, n, m):
    lane = lax.broadcasted_iota(jnp.int32, (n, 128), 1)
    even = ref[pl.ds(row + 2 * m, n, stride=8), :]
    odd = ref[pl.ds(row + 2 * m + 1, n, stride=8), :]
    return jnp.where(lane < 64, pltpu.roll(even, 96, 1), pltpu.roll(odd, 32, 1))


def finish_kernel(x_w, out_ref, y_w):
    lane4 = lax.broadcasted_iota(jnp.int32, (4, 128), 1)
    table = spectral_numbers()
    for v in range(NV):
        parts = [x_w[pl.ds(field_row(m * NV + v), 8), :] for m in range(NI)]
        for n in range(NI):
            total = float(table[0, n]) * parts[0]
            for m in range(1, NI):
                total = total + float(table[m, n]) * parts[m]
            y_w[pl.ds((n * NV + v) * 8, 8), :] = total

    def out_rows(i, c):
        even = y_w[pl.ds(i * 8, 4, stride=2), :]
        odd = y_w[pl.ds(i * 8 + 1, 4, stride=2), :]
        out_ref[i] = jnp.where(lane4 < 64, pltpu.roll(even, 96, 1), pltpu.roll(odd, 32, 1))
        return c

    lax.fori_loop(0, NF, out_rows, 0, unroll=9)


def finish(modes):
    return pl.pallas_call(
        finish_kernel,
        out_shape=jax.ShapeDtypeStruct((NF, 4, 128), jnp.float32),
        scratch_shapes=[pltpu.VMEM((NF * 8, 128), jnp.float32)],
        cost_estimate=pl.CostEstimate(flops=2 * NI * NF * 1024, bytes_accessed=500000, transcendentals=0),
    )(modes).reshape(1, NI, NV, OWN)


def kernel(
    rhs_h, cpl_h, off_h, bm_h, bw_h, don_h, rec_h, gain_h,
    x_w, flag_ref,
    rhs_v, cpl_v, off_v, bm_v, bw_v, gain_v, idx_v,
    wave_w, base_w, edge_s, lane_w,
    send_left, send_right, from_left, from_right,
    code_s, sel_s, xr_s, wr_s, gpk_s, msg_s, got_s,
    in_sem, idx_send, idx_recv, edge_send, edge_recv, msg_send, msg_recv, ready,
):
    r = lax.axis_index("row")
    s = lax.axis_index("space")

    z, p = s // GROUP, s % GROUP

    bar = pltpu.get_barrier_semaphore()

    def greet(row, t):
        pl.semaphore_signal(bar, inc=1, device_id=(row, t), device_id_type=MESH)

    @pl.when(r < ROWS - 1)
    def _():
        for j in range(GROUP):
            greet(r + 1, j * GROUP + p)

    @pl.when(r > 0)
    def _():
        for j in range(GROUP):
            greet(r - 1, j * GROUP + p)

    for j in range(1, GROUP):
        greet(r, z * GROUP + lax.rem(p + j, GROUP))

    @pl.when((p == 0) & (s > 0))
    def _():
        greet(r, s - 1)

    @pl.when((p == GROUP - 1) & (s < NS - 1))
    def _():
        greet(r, s + 1)

    for row in range(ROWS):
        @pl.when((row > r + 1) | (row < r - 1))
        def _():
            greet(row, s)

    loads = [
        pltpu.make_async_copy(bw_h, bw_v, in_sem.at[0]),
        pltpu.make_async_copy(bm_h, bm_v, in_sem.at[1]),
        pltpu.make_async_copy(cpl_h, cpl_v, in_sem.at[2]),
        pltpu.make_async_copy(rhs_h, rhs_v, in_sem.at[3]),
        pltpu.make_async_copy(off_h, off_v, in_sem.at[4]),
        pltpu.make_async_copy(gain_h, gain_v, in_sem.at[5]),
        pltpu.make_async_copy(don_h, idx_v.at[r, 0], in_sem.at[6]),
        pltpu.make_async_copy(rec_h, idx_v.at[r, 1], in_sem.at[7]),
    ]
    for c in loads:
        c.start()

    lane8 = lax.broadcasted_iota(jnp.int32, (8, 128), 1)

    def to_windows(tiles, dst, row):
        n = tiles[0].shape[0]
        lane = lane8[:n]
        up = [pltpu.roll(t, 32, 1) for t in tiles]
        down = [pltpu.roll(t, 96, 1) for t in tiles]
        for m in range(4):
            even = up[m] if m == 0 else jnp.where(lane < 32, up[m - 1], up[m])
            odd = down[m] if m == 3 else jnp.where(lane < 96, down[m], down[m + 1])
            dst[pl.ds(row + 2 * m, n, stride=8), :] = even
            dst[pl.ds(row + 2 * m + 1, n, stride=8), :] = odd

    def pack(firsts, lasts, row):
        n = firsts[0].shape[0]
        lane = lane8[:n]
        left = firsts[0]
        right = pltpu.roll(lasts[0], 32, 1)
        for e in range(1, len(firsts)):
            left = jnp.where(lane >= 32 * e, pltpu.roll(firsts[e], 32 * e, 1), left)
            moved = lasts[e] if e == 3 else pltpu.roll(lasts[e], (32 * e + 32) % 128, 1)
            right = jnp.where(lane >= 32 * e, moved, right)
        send_left[pl.ds(row, n), :] = left
        send_right[pl.ds(row, n), :] = right

    loads[0].wait()

    def wave_units(first, count, row):
        firsts, lasts = [], []
        for e in range(count):
            tiles = [
                jnp.concatenate([bw_v[2 * (first + e) + i, :, pl.ds(128 * m, 128)] for i in range(2)], axis=0)
                for m in range(4)
            ]
            to_windows(tiles, wave_w, (first + e) * 64)
            firsts.append(tiles[0])
            lasts.append(tiles[3])
        pack(firsts, lasts, row)

    def wave_rows(p, c):
        wave_units(4 * p, 4, 8 * p)
        return c

    lax.fori_loop(0, 12, wave_rows, 0, unroll=3)
    wave_units(48, 2, 96)

    for c in loads[1:5]:
        c.wait()
    lane4 = lane8[:4]
    row4 = lax.broadcasted_iota(jnp.int32, (4, 128), 0)
    table = spectral_numbers()
    for v in range(NV):
        parts = [rhs_v[n * NV + v] for n in range(NI)]
        for m in range(NI):
            total = float(table[m, 0]) * parts[0]
            for n in range(1, NI):
                total = total + float(table[m, n]) * parts[n]
            rhs_v[m * NV + v] = total

    for ref, skip, first, count in (
            (bm_v, 0, 0, 25), (cpl_v, 0, 25, 30), (off_v, 0, 55, 6), (rhs_v, 0, 64, 25), (rhs_v, 25, 96, 20)):
        def base_rows(i, c, ref=ref, skip=skip, first=first):
            tile = ref[skip + i].astype(jnp.float32)
            up = pltpu.roll(tile, 32, 1)
            down = pltpu.roll(tile, 96, 1)
            at = (first + i) * 8
            base_w[pl.ds(at, 4, stride=2), :] = jnp.where(lane4 < 32, pltpu.roll(up, 1, 0), up)
            base_w[pl.ds(at + 1, 4, stride=2), :] = jnp.where(lane4 < 96, down, pltpu.roll(down, 3, 0))
            edge_s[0, pl.ds(first + i, 1), :] = tile[0:1]
            edge_s[1, pl.ds(first + i, 1), :] = tile[3:4]
            return c
        lax.fori_loop(0, count, base_rows, 0, unroll=5 if count % 5 == 0 else 6)
    for first, count in ((61, 3), (89, 7), (116, 12)):
        edge_s[:, pl.ds(first, count), :] = jnp.zeros((2, count, 128), jnp.float32)
        base_w[pl.ds(first * 8, count * 8), :] = jnp.zeros((count * 8, 128), jnp.float32)
    for q in range(4):
        pack(
            [edge_s[0, pl.ds(32 * e + 8 * q, 8), :] for e in range(4)],
            [edge_s[1, pl.ds(32 * e + 8 * q, 8), :] for e in range(4)], AT_BASE + 8 * q)
    for c in loads[5:]:
        c.wait()
    xr_s[...] = jnp.zeros(xr_s.shape, jnp.bfloat16)
    x_w[pl.ds(200, 56), :] = jnp.zeros((56, 128), jnp.float32)
    x_w[pl.ds(416, 96), :] = jnp.zeros((96, 128), jnp.float32)

    @pl.when(s == 0)
    def _():
        from_left[...] = jnp.zeros(from_left.shape, jnp.float32)

    @pl.when(s == NS - 1)
    def _():
        from_right[...] = jnp.zeros(from_right.shape, jnp.float32)

    def one_if(condition):
        return jnp.where(condition, 1, 0)

    here = GROUP * (one_if(r > 0) + one_if(r < ROWS - 1)) + GROUP - 1
    here = here + one_if((p == 0) & (s > 0)) + one_if((p == GROUP - 1) & (s < NS - 1))
    here = here + 1 + one_if(r == 0) + one_if(r == ROWS - 1)
    pl.semaphore_wait(bar, here)

    def index_copy(d, part, sem):
        at = idx_v.at[r] if part is None else idx_v.at[r, part]
        return pltpu.make_async_remote_copy(
            at, at, idx_send.at[sem], idx_recv.at[sem],
            device_id=(lax.rem(r + d, ROWS), s), device_id_type=MESH)

    index_copies = [index_copy(ROWS - 1, 1, 0), index_copy(1, None, 1), index_copy(2, None, 2), index_copy(ROWS - 1, 0, 3)]
    index_copies[0].start()
    right = pltpu.make_async_remote_copy(
        send_right, from_left, edge_send.at[0], edge_recv.at[0],
        device_id=(r, lax.rem(s + 1, NS)), device_id_type=MESH)
    left = pltpu.make_async_remote_copy(
        send_left, from_right, edge_send.at[1], edge_recv.at[1],
        device_id=(r, lax.rem(s + NS - 1, NS)), device_id_type=MESH)

    @pl.when(s < NS - 1)
    def _():
        right.start()

    @pl.when(s > 0)
    def _():
        left.start()

    for c in index_copies[1:]:
        c.start()

    @pl.when(r > 0)
    def _():
        for j in range(GROUP):
            pl.semaphore_signal(ready, inc=1, device_id=(r - 1, j * GROUP + p), device_id_type=MESH)

    dev64 = lax.broadcasted_iota(jnp.int32, (NS, 1), 0)
    tri = (lax.broadcasted_iota(jnp.int32, (128, 128), 0) <= lax.broadcasted_iota(jnp.int32, (128, 128), 1))
    tri = tri.astype(jnp.float32).astype(jnp.bfloat16)

    def order(mask):
        before = jnp.zeros((NS, 1), jnp.float32)
        for b in range(NIF // 128):
            m = mask[:, 128 * b:128 * b + 128]
            upto = jnp.dot(m.astype(jnp.bfloat16), tri, preferred_element_type=jnp.float32)
            code_s[:, pl.ds(128 * b, 128)] = jnp.where(m > 0.5, before + upto - 1.0, -1.0)
            before = before + jnp.sum(m, axis=1, keepdims=True)

    def pick(k, value):
        return jnp.sum(jnp.where(code_s[...] == float(k), value, 0.0), axis=1, keepdims=True)

    def in_block(cells, device):
        low = device * OWN
        return (cells >= low) & (cells < low + OWN)

    def in_windows(cells, device):
        low = device * OWN - EDGE
        return (cells >= low) & (cells < low + OWN + 2 * EDGE)

    @pl.when(r < ROWS - 1)
    def _():
        index_copies[0].wait_recv()
        donor = idx_v[r, 0]
        receiver = idx_v[r + 1, 1]
        order((in_block(donor, s) & in_windows(receiver, dev64)).astype(jnp.float32))
        place = (donor - s * OWN + 1).astype(jnp.float32)
        cell = lax.broadcasted_iota(jnp.int32, (NS, OWN), 1).astype(jnp.float32) + 1.0
        for k in range(CAP):
            hit = (pick(k, place) == cell).astype(jnp.float32).astype(jnp.bfloat16)
            sel_s[pl.ds(k * NS, NS), :] = hit

    @pl.when(r > 0)
    def _():
        index_copies[1].wait_recv()
        donor = idx_v[r - 1, 0]
        receiver = idx_v[r, 1]
        order((in_block(donor, dev64) & in_windows(receiver, s)).astype(jnp.float32))
        place = (receiver - s * OWN + EDGE + 1).astype(jnp.float32)
        position = lax.broadcasted_iota(jnp.int32, (NS, 1024), 1)
        cell = ((position // 128) * 64 + position % 128 + 1).astype(jnp.float32)
        lane = lax.broadcasted_iota(jnp.int32, (1, 128), 1)
        field = lane % 32
        for k in range(CAP):
            hit = (pick(k, place) == cell).astype(jnp.float32).astype(jnp.bfloat16)
            wr_s[pl.ds(k * NS, NS), :] = hit
        for k in range(2):
            rows = jnp.zeros((NS, 128), jnp.float32)
            for v in range(NV):
                for g in range(4):
                    mine = (field % NV == v) & (field < 25) & (lane // 32 == g)
                    rows = rows + jnp.where(mine, pick(2 * g + k, gain_v[v]), 0.0)
            gpk_s[pl.ds(k * NS, NS), :] = rows

    @pl.when(s > 0)
    def _():
        right.wait_recv()

    @pl.when(s < NS - 1)
    def _():
        left.wait_recv()

    def merge(dst, row, n, src_row, e):
        lane = lane8[:n]
        low = from_left[pl.ds(src_row, n), :]
        low = low if e == 0 else pltpu.roll(low, 128 - 32 * e, 1)
        high = from_right[pl.ds(src_row, n), :]
        high = high if e == 3 else pltpu.roll(high, 96 - 32 * e, 1)
        at = pl.ds(row, n, stride=8)
        dst[at, :] = jnp.where(lane < 32, low, dst[at, :])
        at = pl.ds(row + 7, n, stride=8)
        dst[at, :] = jnp.where(lane >= 96, high, dst[at, :])

    def wave_edges(p, c):
        for e in range(4):
            merge(wave_w, (4 * p + e) * 64, 8, 8 * p, e)
        return c

    lax.fori_loop(0, 12, wave_edges, 0, unroll=12)
    for e in range(2):
        merge(wave_w, (48 + e) * 64, 8, 96, e)
    for e in range(4):
        for q in range(4 if e < 3 else 3):
            merge(base_w, (32 * e + 8 * q) * 8, 8, AT_BASE + 8 * q, e)

    for j in range(NOFF):
        at = lane8 + base_w[pl.ds((55 + j) * 8, 8), :].astype(jnp.int32)
        lane_w[j] = jnp.clip(at, 0, 127)

    def inflow(h):
        pltpu.make_async_remote_copy(
            msg_s.at[h], got_s.at[h], msg_send.at[h], msg_recv.at[h],
            device_id=(r - 1, s), device_id_type=MESH).wait_recv()
        rows = jnp.concatenate([got_s[h, :, k, :] for k in range(2)], axis=0) * gpk_s[...]
        turned = rows.T
        both = jnp.concatenate([turned[32 * g:32 * g + 32] for g in range(4)], axis=1)
        high = both.astype(jnp.bfloat16)
        low = (both - high.astype(jnp.float32)).astype(jnp.bfloat16)
        added = jnp.dot(jnp.concatenate([high, low], axis=0), wr_s[...], preferred_element_type=jnp.float32)
        added = added[:32] + added[32:]
        for a in range(4 - h):
            for j in range(8):
                at = pl.ds(AT_SOURCE + h * 256 + a * 64 + j, 8, stride=8)
                base_w[at, :] = base_w[at, :] - added[8 * a:8 * a + 8, 128 * j:128 * j + 128]

    def relax(row, count, entry):
        source = [base_w[pl.ds(AT_SOURCE + row + f * 8, 8), :] for f in range(count)]

        def solve(values):
            result = []
            for f in range(count):
                total = None
                for g in range(count):
                    term = entry(f, g) * values[g]
                    total = term if total is None else total + term
                result.append(total)
            return result

        x = solve(source)
        for _ in range(SWEEPS):
            rest = list(source)
            for j in range(NOFF):
                at = lane_w[j]
                for f in range(count):
                    moved = jnp.take_along_axis(x[f], at, axis=1, mode="promise_in_bounds")
                    rest[f] = rest[f] - base_w[pl.ds((25 + j * NV + f % NV) * 8, 8), :] * moved
            x = solve(rest)
        for f in range(count):
            x_w[pl.ds(row + f * 8, 8), :] = x[f]

    def harmonic(k, c):
        row = jnp.where(k < 2, 40 + 80 * k, 256 + 80 * (k - 2))
        relax(row, 10, lambda f, g: wave_w[pl.ds((f * 10 + g) * 32 + k * 8, 8), :])
        return c

    def relax_half(h):
        if h == 0:
            relax(0, NV, lambda f, g: base_w[pl.ds((f * NV + g) * 8, 8), :])
        lax.fori_loop(2 * h, 2 * h + 2, harmonic, 0, unroll=2)

    def donate(h):
        for a in range(2):
            for m in range(4):
                tile = jnp.concatenate(
                    [own_tile(x_w, h * 256 + (2 * a + i) * 64, 8, m) for i in range(2)], axis=0)
                high = tile.astype(jnp.bfloat16)
                low = (tile - high.astype(jnp.float32)).astype(jnp.bfloat16)
                xr_s[pl.ds(16 * a, 16), pl.ds(128 * m, 128)] = high
                xr_s[pl.ds(128 + 16 * a, 16), pl.ds(128 * m, 128)] = low
        values = lax.dot_general(
            sel_s[...], xr_s[...], (((1,), (1,)), ((), ())), preferred_element_type=jnp.float32)
        values = values[:, :128] + values[:, 128:]
        for k in range(2):
            rows = values[k * NS:(k + 1) * NS]
            for g in range(1, 4):
                at = (2 * g + k) * NS
                rows = rows + pltpu.roll(values[at:at + NS], 32 * g, 1)
            msg_s[h, :, k, :] = rows
        if h == 0:
            pl.semaphore_wait(ready, GROUP)

        for d in (4, 3, 5, 2, 6, 1, 7, 0):
            plane = lax.rem(z + d, GROUP) * GROUP
            for j in range(GROUP):
                t = plane + j
                pltpu.make_async_remote_copy(
                    msg_s.at[h, t], got_s.at[h, s], msg_send.at[h], msg_recv.at[h],
                    device_id=(r + 1, t), device_id_type=MESH).start()

    for h in range(2):
        @pl.when(r > 0)
        def _():
            inflow(h)

        relax_half(h)

        @pl.when(r < ROWS - 1)
        def _():
            donate(h)

    @pl.when(r == ROWS - 1)
    def _():
        index_copies[0].wait_recv()

    @pl.when(r == 0)
    def _():
        index_copies[1].wait_recv()

    index_copies[2].wait_recv()
    index_copies[3].wait_recv()
    for c in index_copies:
        c.wait_send()
    most = jnp.zeros((NS, NS), jnp.float32)
    for row in range(ROWS - 1):
        gives = in_block(idx_v[row, 0], dev64).astype(jnp.float32).astype(jnp.bfloat16)
        takes = in_windows(idx_v[row + 1, 1], dev64).astype(jnp.float32).astype(jnp.bfloat16)
        count = lax.dot_general(gives, takes, (((1,), (1,)), ((), ())), preferred_element_type=jnp.float32)
        most = jnp.maximum(most, count)
    flag_ref[0, 0] = jnp.where(jnp.max(most) > CAP + 0.5, 1, 0)

    @pl.when(s < NS - 1)
    def _():
        right.wait_send()

    @pl.when(s > 0)
    def _():
        left.wait_send()

    @pl.when(r < ROWS - 1)
    def _():
        for h in range(2):
            pltpu.make_async_remote_copy(
                msg_s.at[h], got_s.at[h], msg_send.at[h], msg_recv.at[h],
                device_id=(r + 1, s), device_id_type=MESH).wait_send()


def fast(rhs, cpl, off, bm, bw, don, rec, gain):
    bw = jnp.transpose(bw, (0, 2, 3, 1, 4)).reshape(100, 4, OWN)
    rhs, cpl, off, bm = (a.reshape(-1, 4, 128) for a in (rhs, cpl, off, bm))
    gain = gain.reshape(NV, 1, NIF)
    any_space = pl.BlockSpec(memory_space=pl.ANY)
    vmem = pl.BlockSpec(memory_space=pltpu.VMEM)
    f32, i32, bf16 = jnp.float32, jnp.int32, jnp.bfloat16
    return pl.pallas_call(
        kernel,
        out_shape=(jax.ShapeDtypeStruct((512, 128), f32), jax.ShapeDtypeStruct((1, 1), i32)),
        in_specs=[any_space] * 8,
        out_specs=(vmem, pl.BlockSpec(memory_space=pltpu.SMEM)),
        scratch_shapes=[
            pltpu.VMEM((NF, 4, 128), f32),
            pltpu.VMEM((NOFF * NV, 4, 128), f32),
            pltpu.VMEM((NOFF, 4, 128), i32),
            pltpu.VMEM((NV * NV, 4, 128), f32),
            pltpu.VMEM((100, 4, OWN), f32),
            pltpu.VMEM((NV, 1, NIF), f32),
            pltpu.VMEM((ROWS, 2, 1, NIF), i32),
            pltpu.VMEM((3200, 128), f32),
            pltpu.VMEM((1024, 128), f32),
            pltpu.VMEM((2, 128, 128), f32),
            pltpu.VMEM((NOFF, 8, 128), i32),
            pltpu.VMEM((HALO_ROWS, 128), f32),
            pltpu.VMEM((HALO_ROWS, 128), f32),
            pltpu.VMEM((HALO_ROWS, 128), f32),
            pltpu.VMEM((HALO_ROWS, 128), f32),
            pltpu.VMEM((NS, NIF), f32),
            pltpu.VMEM((CAP * NS, OWN), bf16),
            pltpu.VMEM((256, OWN), bf16),
            pltpu.VMEM((CAP * NS, 1024), bf16),
            pltpu.VMEM((2 * NS, 128), f32),
            pltpu.VMEM((2, NS, 2, 128), f32),
            pltpu.VMEM((2, NS, 2, 128), f32),
            pltpu.SemaphoreType.DMA((8,)),
            pltpu.SemaphoreType.DMA((ROWS,)),
            pltpu.SemaphoreType.DMA((ROWS,)),
            pltpu.SemaphoreType.DMA((2,)),
            pltpu.SemaphoreType.DMA((2,)),
            pltpu.SemaphoreType.DMA((2,)),
            pltpu.SemaphoreType.DMA((2,)),
            pltpu.SemaphoreType.REGULAR,
        ],
        compiler_params=pltpu.CompilerParams(
            collective_id=0, has_side_effects=True, vmem_limit_bytes=40 * 1024 * 1024),
    )(rhs, cpl, off, bm, bw, don, rec, gain)


def with_halo(block, sides, width):
    for axis, dim in sides:
        count = lax.axis_size(axis)
        forward = [(i, i + 1) for i in range(count - 1)]
        backward = [(target, source) for source, target in forward]
        low = lax.ppermute(
            lax.slice_in_dim(block, block.shape[dim] - width, None, axis=dim), axis, forward
        )
        high = lax.ppermute(lax.slice_in_dim(block, 0, width, axis=dim), axis, backward)
        block = jnp.concatenate([low, block, high], axis=dim)
    return block


def from_behind(value, axis, steps):
    count = lax.axis_size(axis)
    first, last = (max(0, -steps), min(count, count - steps))
    return lax.ppermute(value, axis, [(source, source + steps) for source in range(first, last)])


def sum_over(value, axis):
    count = lax.axis_size(axis)
    step = 1
    while step < count:
        value = value + lax.ppermute(value, axis, [(i, i ^ step) for i in range(count)])
        step *= 2
    return value


def spectral_table(instances):
    position = jnp.arange(instances).astype(jnp.float32)
    harmonic = jnp.arange(1, (instances - 1) // 2 + 1).astype(jnp.float32)
    phase_angle = 2.0 * math.pi / instances * harmonic[:, None] * position[None, :]
    weight = math.sqrt(2.0 / instances)
    wave_rows = jnp.stack(
        [weight * jnp.cos(phase_angle), weight * jnp.sin(phase_angle)], axis=1
    ).reshape(-1, instances)
    mean_row = jnp.full((1, instances), 1.0 / math.sqrt(instances), jnp.float32)
    return jnp.concatenate([mean_row, wave_rows], axis=0)


def invert_blocks(values, block_mean, block_wave, spectral):
    spectral_modes = jnp.einsum("kn,nvc->kvc", spectral, values, precision=lax.Precision.HIGHEST)
    variables = spectral_modes.shape[1]
    harmonics = (spectral_modes.shape[0] - 1) // 2
    steady = jnp.sum(block_mean * spectral_modes[0][None, :, :], axis=1)
    paired = spectral_modes[1:].reshape(harmonics, 2 * variables, spectral_modes.shape[2])
    paired = jnp.sum(block_wave * paired[:, None, :, :], axis=2)
    joined = jnp.concatenate(
        [steady[None], paired.reshape(2 * harmonics, variables, spectral_modes.shape[2])], axis=0
    )
    return jnp.einsum("kn,kvc->nvc", spectral, joined, precision=lax.Precision.HIGHEST)


def neighbor_sum(padded, offsets, coupling, reach_cells):
    cell_count = offsets.shape[1]
    cell_base = jnp.arange(cell_count, dtype=jnp.int32) + reach_cells
    accumulated = jnp.zeros((padded.shape[0], padded.shape[1], cell_count), jnp.float32)
    for neighbor in range(offsets.shape[0]):
        neighbor_vals = jnp.take(padded, cell_base + offsets[neighbor], axis=2)
        accumulated = accumulated + coupling[neighbor][None, :, :] * neighbor_vals
    return accumulated


def general(
    right_side, coupling, offsets, block_mean, block_wave, donor_cells, receiver_cells, inlet_gain
):
    space_rank = lax.axis_index("space")
    source_base = right_side[0]
    cell_count = source_base.shape[2]
    spectral = spectral_table(source_base.shape[0])
    first_cell = space_rank * cell_count
    mean_blocks = block_mean[0]
    wave_blocks = block_wave[0]

    def apply_inverse(values):
        return invert_blocks(values, mean_blocks, wave_blocks, spectral)

    donor_local = donor_cells[0] - first_cell
    donor_inside = ((donor_local >= 0) & (donor_local < cell_count)).astype(jnp.float32)
    donor_clip = jnp.clip(donor_local, 0, cell_count - 1)
    receiver_local = receiver_cells[0] - first_cell
    receiver_inside = ((receiver_local >= 0) & (receiver_local < cell_count)).astype(jnp.float32)
    receiver_clip = jnp.clip(receiver_local, 0, cell_count - 1)
    row_total = lax.axis_size("row")
    inlet_profile = jnp.zeros((NI, NV, NIF), jnp.float32)

    def row(_, carry):
        inlet_profile, _ = carry
        inflow = inlet_gain[0][None, :, :] * inlet_profile * receiver_inside[None, None, :]
        source = source_base - jnp.zeros_like(source_base).at[:, :, receiver_clip].add(inflow)

        def sweep(_, state):
            padded = with_halo(state, (("space", 2),), HALO)
            coupled = neighbor_sum(padded, offsets[0], coupling[0], HALO)
            return apply_inverse(source - coupled)

        state_field = lax.fori_loop(0, SWEEPS, sweep, apply_inverse(source))
        outgoing = jnp.take(state_field, donor_clip, axis=2) * donor_inside[None, None, :]
        return from_behind(sum_over(outgoing, "space"), "row", 1), state_field

    return lax.fori_loop(0, row_total, row, (inlet_profile, source_base))[1][None]


def on_device(*args):
    modes, flag = fast(*args)
    return lax.cond(flag[0, 0] > 0, lambda: general(*args), lambda: finish(modes))


def solution(mesh):
    return jax.shard_map(
        on_device,
        mesh=mesh,
        in_specs=(
            P("row", None, None, "space"),
            P("row", None, None, "space"),
            P("row", None, "space"),
            P("row", None, None, "space"),
            P("row", None, None, None, "space"),
            P("row", None),
            P("row", None),
            P("row", None, None),
        ),
        out_specs=P("row", None, None, "space"),
        check_vma=False,
    )
```

```python
import functools
import math

import jax
import jax.numpy as jnp
import numpy as np
from jax import lax
from jax.experimental import pallas as pl
from jax.experimental.pallas import tpu as pltpu
from jax.sharding import PartitionSpec as P

NI = 9
NV = 5
NF = NI * NV
NOFF = 6
HALO = 16
SWEEPS = 2
NIF = 1024
ROWS = 4
NS = 64
GROUP = 8
FAR = (4, 3, 5, 2, 6, 1, 7, 0)
OWN = 512
EDGE = 32
CAP = 6
MESH = pl.DeviceIdType.MESH

HALO_ROWS = 136
AT_BASE = 104
AT_SOURCE = 512


def field_row(f):
    return (f if f < 25 else f + 7) * 8


def spectral_numbers():
    n = np.arange(NI, dtype=np.float64)
    table = [np.full(NI, 1.0 / math.sqrt(NI))]
    for k in range(1, (NI - 1) // 2 + 1):
        table.append(math.sqrt(2.0 / NI) * np.cos(2.0 * math.pi * k * n / NI))
        table.append(math.sqrt(2.0 / NI) * np.sin(2.0 * math.pi * k * n / NI))
    return np.stack(table).astype(np.float32)


def own_tile(ref, row, n, m):
    lane = lax.broadcasted_iota(jnp.int32, (n, 128), 1)
    even = ref[pl.ds(row + 2 * m, n, stride=8), :]
    odd = ref[pl.ds(row + 2 * m + 1, n, stride=8), :]
    return jnp.where(lane < 64, pltpu.roll(even, 96, 1), pltpu.roll(odd, 32, 1))


def finish_kernel(x_w, out_ref, y_w):
    lane4 = lax.broadcasted_iota(jnp.int32, (4, 128), 1)
    table = spectral_numbers()
    for v in range(NV):
        parts = [x_w[pl.ds(field_row(m * NV + v), 8), :] for m in range(NI)]
        for n in range(NI):
            total = float(table[0, n]) * parts[0]
            for m in range(1, NI):
                total = total + float(table[m, n]) * parts[m]
            y_w[pl.ds((n * NV + v) * 8, 8), :] = total

    def out_rows(i, c):
        even = y_w[pl.ds(i * 8, 4, stride=2), :]
        odd = y_w[pl.ds(i * 8 + 1, 4, stride=2), :]
        out_ref[i] = jnp.where(lane4 < 64, pltpu.roll(even, 96, 1), pltpu.roll(odd, 32, 1))
        return c

    lax.fori_loop(0, NF, out_rows, 0, unroll=9)


def finish(modes):
    return pl.pallas_call(
        finish_kernel,
        out_shape=jax.ShapeDtypeStruct((NF, 4, 128), jnp.float32),
        scratch_shapes=[pltpu.VMEM((NF * 8, 128), jnp.float32)],
        cost_estimate=pl.CostEstimate(flops=2 * NI * NF * 1024, bytes_accessed=500000, transcendentals=0),
    )(modes).reshape(1, NI, NV, OWN)


def kernel(
    rhs_h, cpl_h, off_h, bm_h, bw_h, don_h, rec_h, gain_h,
    x_w, flag_ref,
    rhs_v, cpl_v, off_v, bm_v, bw_v, gain_v, idx_v,
    wave_w, base_w, edge_s, lane_w,
    send_left, send_right, from_left, from_right,
    code_s, sel_s, xr_s, wr_s, gpk_s, msg_s, got_s,
    in_sem, idx_send, idx_recv, edge_send, edge_recv, msg_send, msg_recv, ready,
):
    r = lax.axis_index("row")
    s = lax.axis_index("space")

    z, p = s // GROUP, s % GROUP

    bar = pltpu.get_barrier_semaphore()

    def greet(row, t):
        pl.semaphore_signal(bar, inc=1, device_id=(row, t), device_id_type=MESH)

    @pl.when(r < ROWS - 1)
    def _():
        for j in range(GROUP):
            greet(r + 1, z * GROUP + j)

    @pl.when(r > 0)
    def _():
        for j in range(GROUP):
            greet(r - 1, z * GROUP + j)

    for d in FAR[:-1]:
        greet(r, lax.rem(z + d, GROUP) * GROUP + p)

    @pl.when(s > 0)
    def _():
        greet(r, s - 1)

    @pl.when(s < NS - 1)
    def _():
        greet(r, s + 1)

    for row in range(ROWS):
        @pl.when((row > r + 1) | (row < r - 1))
        def _():
            greet(row, s)

    loads = [
        pltpu.make_async_copy(bw_h, bw_v, in_sem.at[0]),
        pltpu.make_async_copy(bm_h, bm_v, in_sem.at[1]),
        pltpu.make_async_copy(cpl_h, cpl_v, in_sem.at[2]),
        pltpu.make_async_copy(rhs_h, rhs_v, in_sem.at[3]),
        pltpu.make_async_copy(off_h, off_v, in_sem.at[4]),
        pltpu.make_async_copy(gain_h, gain_v, in_sem.at[5]),
        pltpu.make_async_copy(don_h, idx_v.at[r, 0], in_sem.at[6]),
        pltpu.make_async_copy(rec_h, idx_v.at[r, 1], in_sem.at[7]),
    ]
    for c in loads:
        c.start()

    lane8 = lax.broadcasted_iota(jnp.int32, (8, 128), 1)

    def to_windows(tiles, dst, row):
        n = tiles[0].shape[0]
        lane = lane8[:n]
        up = [pltpu.roll(t, 32, 1) for t in tiles]
        down = [pltpu.roll(t, 96, 1) for t in tiles]
        for m in range(4):
            even = up[m] if m == 0 else jnp.where(lane < 32, up[m - 1], up[m])
            odd = down[m] if m == 3 else jnp.where(lane < 96, down[m], down[m + 1])
            dst[pl.ds(row + 2 * m, n, stride=8), :] = even
            dst[pl.ds(row + 2 * m + 1, n, stride=8), :] = odd

    def pack(firsts, lasts, row):
        n = firsts[0].shape[0]
        lane = lane8[:n]
        left = firsts[0]
        right = pltpu.roll(lasts[0], 32, 1)
        for e in range(1, len(firsts)):
            left = jnp.where(lane >= 32 * e, pltpu.roll(firsts[e], 32 * e, 1), left)
            moved = lasts[e] if e == 3 else pltpu.roll(lasts[e], (32 * e + 32) % 128, 1)
            right = jnp.where(lane >= 32 * e, moved, right)
        send_left[pl.ds(row, n), :] = left
        send_right[pl.ds(row, n), :] = right

    loads[0].wait()

    def wave_tile(u, m):
        return jnp.concatenate([bw_v[2 * u + i, :, pl.ds(128 * m, 128)] for i in range(2)], axis=0)

    def wave_pack(p, c):
        pack([wave_tile(4 * p + e, 0) for e in range(4)], [wave_tile(4 * p + e, 3) for e in range(4)], 8 * p)
        return c

    lax.fori_loop(0, 12, wave_pack, 0, unroll=4)
    pack([wave_tile(48 + e, 0) for e in range(2)], [wave_tile(48 + e, 3) for e in range(2)], 96)

    for c in loads[1:5]:
        c.wait()
    table = spectral_numbers()
    for v in range(NV):
        parts = [rhs_v[n * NV + v] for n in range(NI)]
        for m in range(NI):
            total = float(table[m, 0]) * parts[0]
            for n in range(1, NI):
                total = total + float(table[m, n]) * parts[n]
            rhs_v[m * NV + v] = total

    base_parts = (
        (bm_v, 0, 0, 25), (cpl_v, 0, 25, 30), (off_v, 0, 55, 6), (rhs_v, 0, 64, 25), (rhs_v, 25, 96, 20))
    for ref, skip, first, count in base_parts:
        for i in range(count):
            tile = ref[skip + i].astype(jnp.float32)
            edge_s[0, pl.ds(first + i, 1), :] = tile[0:1]
            edge_s[1, pl.ds(first + i, 1), :] = tile[3:4]
    for first, count in ((61, 3), (89, 7), (116, 12)):
        edge_s[:, pl.ds(first, count), :] = jnp.zeros((2, count, 128), jnp.float32)
        base_w[pl.ds(first * 8, count * 8), :] = jnp.zeros((count * 8, 128), jnp.float32)
    for q in range(4):
        pack(
            [edge_s[0, pl.ds(32 * e + 8 * q, 8), :] for e in range(4)],
            [edge_s[1, pl.ds(32 * e + 8 * q, 8), :] for e in range(4)], AT_BASE + 8 * q)
    for c in loads[5:]:
        c.wait()
    xr_s[...] = jnp.zeros(xr_s.shape, jnp.bfloat16)
    x_w[pl.ds(200, 56), :] = jnp.zeros((56, 128), jnp.float32)
    x_w[pl.ds(416, 96), :] = jnp.zeros((96, 128), jnp.float32)

    @pl.when(s == 0)
    def _():
        from_left[...] = jnp.zeros(from_left.shape, jnp.float32)

    @pl.when(s == NS - 1)
    def _():
        from_right[...] = jnp.zeros(from_right.shape, jnp.float32)

    def one_if(condition):
        return jnp.where(condition, 1, 0)

    here = GROUP * (one_if(r > 0) + one_if(r < ROWS - 1)) + GROUP - 1
    here = here + one_if(s > 0) + one_if(s < NS - 1)
    here = here + 1 + one_if(r == 0) + one_if(r == ROWS - 1)
    pl.semaphore_wait(bar, here)

    @pl.when(r > 0)
    def _():
        for j in range(GROUP):
            at = (r - 1, z * GROUP + j)
            pl.semaphore_signal(ready, inc=1, device_id=at, device_id_type=MESH)

    def index_copy(d, part, sem):
        at = idx_v.at[r] if part is None else idx_v.at[r, part]
        return pltpu.make_async_remote_copy(
            at, at, idx_send.at[sem], idx_recv.at[sem],
            device_id=(lax.rem(r + d, ROWS), s), device_id_type=MESH)

    index_copies = [index_copy(ROWS - 1, 1, 0), index_copy(1, None, 1), index_copy(2, None, 2), index_copy(ROWS - 1, 0, 3)]
    index_copies[0].start()
    right = pltpu.make_async_remote_copy(
        send_right, from_left, edge_send.at[0], edge_recv.at[0],
        device_id=(r, lax.rem(s + 1, NS)), device_id_type=MESH)
    left = pltpu.make_async_remote_copy(
        send_left, from_right, edge_send.at[1], edge_recv.at[1],
        device_id=(r, lax.rem(s + NS - 1, NS)), device_id_type=MESH)

    @pl.when(s < NS - 1)
    def _():
        right.start()

    @pl.when(s > 0)
    def _():
        left.start()

    for c in index_copies[1:]:
        c.start()

    def wave_windows(u, c):
        to_windows([wave_tile(u, m) for m in range(4)], wave_w, u * 64)
        return c

    lax.fori_loop(0, 50, wave_windows, 0, unroll=10)
    lane4 = lane8[:4]
    for ref, skip, first, count in base_parts:
        def base_rows(i, c, ref=ref, skip=skip, first=first):
            tile = ref[skip + i].astype(jnp.float32)
            up = pltpu.roll(tile, 32, 1)
            down = pltpu.roll(tile, 96, 1)
            at = (first + i) * 8
            base_w[pl.ds(at, 4, stride=2), :] = jnp.where(lane4 < 32, pltpu.roll(up, 1, 0), up)
            base_w[pl.ds(at + 1, 4, stride=2), :] = jnp.where(lane4 < 96, down, pltpu.roll(down, 3, 0))
            return c
        lax.fori_loop(0, count, base_rows, 0, unroll=5 if count % 5 == 0 else 6)

    dev64 = lax.broadcasted_iota(jnp.int32, (NS, 1), 0)
    tri = (lax.broadcasted_iota(jnp.int32, (128, 128), 0) <= lax.broadcasted_iota(jnp.int32, (128, 128), 1))
    tri = tri.astype(jnp.float32).astype(jnp.bfloat16)

    def order(mask):
        before = jnp.zeros((NS, 1), jnp.float32)
        for b in range(NIF // 128):
            m = mask[:, 128 * b:128 * b + 128]
            upto = jnp.dot(m.astype(jnp.bfloat16), tri, preferred_element_type=jnp.float32)
            code_s[:, pl.ds(128 * b, 128)] = jnp.where(m > 0.5, before + upto - 1.0, -1.0)
            before = before + jnp.sum(m, axis=1, keepdims=True)

    def pick(k, value):
        return jnp.sum(jnp.where(code_s[...] == float(k), value, 0.0), axis=1, keepdims=True)

    def in_block(cells, device):
        low = device * OWN
        return (cells >= low) & (cells < low + OWN)

    def in_windows(cells, device):
        low = device * OWN - EDGE
        return (cells >= low) & (cells < low + OWN + 2 * EDGE)

    @pl.when(r < ROWS - 1)
    def _():
        index_copies[0].wait_recv()
        donor = idx_v[r, 0]
        receiver = idx_v[r + 1, 1]
        order((in_block(donor, s) & in_windows(receiver, dev64)).astype(jnp.float32))
        place = (donor - s * OWN + 1).astype(jnp.float32)
        cell = lax.broadcasted_iota(jnp.int32, (NS, OWN), 1).astype(jnp.float32) + 1.0
        for k in range(CAP):
            hit = (pick(k, place) == cell).astype(jnp.float32).astype(jnp.bfloat16)
            sel_s[pl.ds(k * NS, NS), :] = hit

    @pl.when(r > 0)
    def _():
        index_copies[1].wait_recv()
        donor = idx_v[r - 1, 0]
        receiver = idx_v[r, 1]
        order((in_block(donor, dev64) & in_windows(receiver, s)).astype(jnp.float32))
        place = (receiver - s * OWN + EDGE + 1).astype(jnp.float32)
        position = lax.broadcasted_iota(jnp.int32, (NS, 1024), 1)
        cell = ((position // 128) * 64 + position % 128 + 1).astype(jnp.float32)
        lane = lax.broadcasted_iota(jnp.int32, (1, 128), 1)
        field = lane % 32
        for k in range(CAP):
            hit = (pick(k, place) == cell).astype(jnp.float32).astype(jnp.bfloat16)
            wr_s[pl.ds(k * NS, NS), :] = hit
        for k in range(2):
            rows = jnp.zeros((NS, 128), jnp.float32)
            for v in range(NV):
                for g in range(CAP // 2):
                    mine = (field % NV == v) & (field < 25) & (lane // 32 == g)
                    rows = rows + jnp.where(mine, pick(2 * g + k, gain_v[v]), 0.0)
            gpk_s[pl.ds(k * NS, NS), :] = rows

    @pl.when(s > 0)
    def _():
        right.wait_recv()

    @pl.when(s < NS - 1)
    def _():
        left.wait_recv()

    def merge(dst, row, n, src_row, e):
        lane = lane8[:n]
        low = from_left[pl.ds(src_row, n), :]
        low = low if e == 0 else pltpu.roll(low, 128 - 32 * e, 1)
        high = from_right[pl.ds(src_row, n), :]
        high = high if e == 3 else pltpu.roll(high, 96 - 32 * e, 1)
        at = pl.ds(row, n, stride=8)
        dst[at, :] = jnp.where(lane < 32, low, dst[at, :])
        at = pl.ds(row + 7, n, stride=8)
        dst[at, :] = jnp.where(lane >= 96, high, dst[at, :])

    def wave_edges(p, c):
        for e in range(4):
            merge(wave_w, (4 * p + e) * 64, 8, 8 * p, e)
        return c

    lax.fori_loop(0, 12, wave_edges, 0, unroll=12)
    for e in range(2):
        merge(wave_w, (48 + e) * 64, 8, 96, e)
    for e in range(4):
        for q in range(4 if e < 3 else 3):
            merge(base_w, (32 * e + 8 * q) * 8, 8, AT_BASE + 8 * q, e)

    for j in range(NOFF):
        at = lane8 + base_w[pl.ds((55 + j) * 8, 8), :].astype(jnp.int32)
        lane_w[j] = jnp.clip(at, 0, 127)

    def inflow(h):
        pltpu.make_async_remote_copy(
            msg_s.at[h], got_s.at[h], msg_send.at[h], msg_recv.at[h],
            device_id=(r - 1, s), device_id_type=MESH).wait_recv()
        rows = jnp.concatenate([got_s[h, :, k, :] for k in range(2)], axis=0) * gpk_s[...]
        turned = rows.T
        both = jnp.concatenate([turned[32 * g:32 * g + 32] for g in range(CAP // 2)], axis=1)
        high = both.astype(jnp.bfloat16)
        low = (both - high.astype(jnp.float32)).astype(jnp.bfloat16)
        added = jnp.dot(jnp.concatenate([high, low], axis=0), wr_s[...], preferred_element_type=jnp.float32)
        added = added[:32] + added[32:]
        for a in range(4 - h):
            for j in range(8):
                at = pl.ds(AT_SOURCE + h * 256 + a * 64 + j, 8, stride=8)
                base_w[at, :] = base_w[at, :] - added[8 * a:8 * a + 8, 128 * j:128 * j + 128]

    def relax(row, count, entry):
        source = [base_w[pl.ds(AT_SOURCE + row + f * 8, 8), :] for f in range(count)]

        def solve(values):
            result = []
            for f in range(count):
                total = None
                for g in range(count):
                    term = entry(f, g) * values[g]
                    total = term if total is None else total + term
                result.append(total)
            return result

        x = solve(source)
        for _ in range(SWEEPS):
            rest = list(source)
            for j in range(NOFF):
                at = lane_w[j]
                for f in range(count):
                    moved = jnp.take_along_axis(x[f], at, axis=1, mode="promise_in_bounds")
                    rest[f] = rest[f] - base_w[pl.ds((25 + j * NV + f % NV) * 8, 8), :] * moved
            x = solve(rest)
        for f in range(count):
            x_w[pl.ds(row + f * 8, 8), :] = x[f]

    def harmonic(k, c):
        row = 40 + 80 * k if k < 2 else 256 + 80 * (k - 2)
        relax(row, 10, lambda f, g: wave_w[pl.ds((f * 10 + g) * 32 + k * 8, 8), :])
        return c

    def relax_half(h):
        if h == 0:
            relax(0, NV, lambda f, g: base_w[pl.ds((f * NV + g) * 8, 8), :])
        for k in (2 * h, 2 * h + 1):
            harmonic(k, 0)

    def donate(h):
        for a in range(2):
            for m in range(4):
                tile = jnp.concatenate(
                    [own_tile(x_w, h * 256 + (2 * a + i) * 64, 8, m) for i in range(2)], axis=0)
                high = tile.astype(jnp.bfloat16)
                low = (tile - high.astype(jnp.float32)).astype(jnp.bfloat16)
                xr_s[pl.ds(16 * a, 16), pl.ds(128 * m, 128)] = high
                xr_s[pl.ds(128 + 16 * a, 16), pl.ds(128 * m, 128)] = low
        values = lax.dot_general(
            sel_s[...], xr_s[...], (((1,), (1,)), ((), ())), preferred_element_type=jnp.float32)
        values = values[:, :128] + values[:, 128:]
        for k in range(2):
            rows = values[k * NS:(k + 1) * NS]
            for g in range(1, CAP // 2):
                at = (2 * g + k) * NS
                rows = rows + pltpu.roll(values[at:at + NS], 32 * g, 1)
            msg_s[h, :, k, :] = rows
        if h == 0:
            pl.semaphore_wait(ready, GROUP)

        for d in FAR:
            plane = lax.rem(z + d, GROUP) * GROUP
            for j in range(GROUP):
                t = plane + j
                pltpu.make_async_remote_copy(
                    msg_s.at[h, t], got_s.at[h, s], msg_send.at[h], msg_recv.at[h],
                    device_id=(r + 1, t), device_id_type=MESH).start()

    for h in range(2):
        @pl.when(r > 0)
        def _():
            inflow(h)

        relax_half(h)

        @pl.when(r < ROWS - 1)
        def _():
            donate(h)

    @pl.when(r == ROWS - 1)
    def _():
        index_copies[0].wait_recv()

    @pl.when(r == 0)
    def _():
        index_copies[1].wait_recv()

    index_copies[2].wait_recv()
    index_copies[3].wait_recv()
    for c in index_copies:
        c.wait_send()
    most = jnp.zeros((NS, NS), jnp.float32)
    for row in range(ROWS - 1):
        gives = in_block(idx_v[row, 0], dev64).astype(jnp.float32).astype(jnp.bfloat16)
        takes = in_windows(idx_v[row + 1, 1], dev64).astype(jnp.float32).astype(jnp.bfloat16)
        count = lax.dot_general(gives, takes, (((1,), (1,)), ((), ())), preferred_element_type=jnp.float32)
        most = jnp.maximum(most, count)
    flag_ref[0, 0] = jnp.where(jnp.max(most) > CAP + 0.5, 1, 0)

    @pl.when(s < NS - 1)
    def _():
        right.wait_send()

    @pl.when(s > 0)
    def _():
        left.wait_send()

    @pl.when(r < ROWS - 1)
    def _():
        for h in range(2):
            pltpu.make_async_remote_copy(
                msg_s.at[h], got_s.at[h], msg_send.at[h], msg_recv.at[h],
                device_id=(r + 1, s), device_id_type=MESH).wait_send()


def fast(rhs, cpl, off, bm, bw, don, rec, gain):
    bw = jnp.transpose(bw, (0, 2, 3, 1, 4)).reshape(100, 4, OWN)
    rhs, cpl, off, bm = (a.reshape(-1, 4, 128) for a in (rhs, cpl, off, bm))
    gain = gain.reshape(NV, 1, NIF)
    any_space = pl.BlockSpec(memory_space=pl.ANY)
    vmem = pl.BlockSpec(memory_space=pltpu.VMEM)
    f32, i32, bf16 = jnp.float32, jnp.int32, jnp.bfloat16
    return pl.pallas_call(
        kernel,
        out_shape=(jax.ShapeDtypeStruct((512, 128), f32), jax.ShapeDtypeStruct((1, 1), i32)),
        in_specs=[any_space] * 8,
        out_specs=(vmem, pl.BlockSpec(memory_space=pltpu.SMEM)),
        scratch_shapes=[
            pltpu.VMEM((NF, 4, 128), f32),
            pltpu.VMEM((NOFF * NV, 4, 128), f32),
            pltpu.VMEM((NOFF, 4, 128), i32),
            pltpu.VMEM((NV * NV, 4, 128), f32),
            pltpu.VMEM((100, 4, OWN), f32),
            pltpu.VMEM((NV, 1, NIF), f32),
            pltpu.VMEM((ROWS, 2, 1, NIF), i32),
            pltpu.VMEM((3200, 128), f32),
            pltpu.VMEM((1024, 128), f32),
            pltpu.VMEM((2, 128, 128), f32),
            pltpu.VMEM((NOFF, 8, 128), i32),
            pltpu.VMEM((HALO_ROWS, 128), f32),
            pltpu.VMEM((HALO_ROWS, 128), f32),
            pltpu.VMEM((HALO_ROWS, 128), f32),
            pltpu.VMEM((HALO_ROWS, 128), f32),
            pltpu.VMEM((NS, NIF), f32),
            pltpu.VMEM((CAP * NS, OWN), bf16),
            pltpu.VMEM((256, OWN), bf16),
            pltpu.VMEM((CAP * NS, 1024), bf16),
            pltpu.VMEM((2 * NS, 128), f32),
            pltpu.VMEM((2, NS, 2, 128), f32),
            pltpu.VMEM((2, NS, 2, 128), f32),
            pltpu.SemaphoreType.DMA((8,)),
            pltpu.SemaphoreType.DMA((ROWS,)),
            pltpu.SemaphoreType.DMA((ROWS,)),
            pltpu.SemaphoreType.DMA((2,)),
            pltpu.SemaphoreType.DMA((2,)),
            pltpu.SemaphoreType.DMA((2,)),
            pltpu.SemaphoreType.DMA((2,)),
            pltpu.SemaphoreType.REGULAR,
        ],
        compiler_params=pltpu.CompilerParams(
            collective_id=0, has_side_effects=True, vmem_limit_bytes=40 * 1024 * 1024),
    )(rhs, cpl, off, bm, bw, don, rec, gain)


def with_halo(block, sides, width):
    for axis, dim in sides:
        count = lax.axis_size(axis)
        forward = [(i, i + 1) for i in range(count - 1)]
        backward = [(target, source) for source, target in forward]
        low = lax.ppermute(
            lax.slice_in_dim(block, block.shape[dim] - width, None, axis=dim), axis, forward
        )
        high = lax.ppermute(lax.slice_in_dim(block, 0, width, axis=dim), axis, backward)
        block = jnp.concatenate([low, block, high], axis=dim)
    return block


def from_behind(value, axis, steps):
    count = lax.axis_size(axis)
    first, last = (max(0, -steps), min(count, count - steps))
    return lax.ppermute(value, axis, [(source, source + steps) for source in range(first, last)])


def sum_over(value, axis):
    count = lax.axis_size(axis)
    step = 1
    while step < count:
        value = value + lax.ppermute(value, axis, [(i, i ^ step) for i in range(count)])
        step *= 2
    return value


def spectral_table(instances):
    position = jnp.arange(instances).astype(jnp.float32)
    harmonic = jnp.arange(1, (instances - 1) // 2 + 1).astype(jnp.float32)
    phase_angle = 2.0 * math.pi / instances * harmonic[:, None] * position[None, :]
    weight = math.sqrt(2.0 / instances)
    wave_rows = jnp.stack(
        [weight * jnp.cos(phase_angle), weight * jnp.sin(phase_angle)], axis=1
    ).reshape(-1, instances)
    mean_row = jnp.full((1, instances), 1.0 / math.sqrt(instances), jnp.float32)
    return jnp.concatenate([mean_row, wave_rows], axis=0)


def invert_blocks(values, block_mean, block_wave, spectral):
    spectral_modes = jnp.einsum("kn,nvc->kvc", spectral, values, precision=lax.Precision.HIGHEST)
    variables = spectral_modes.shape[1]
    harmonics = (spectral_modes.shape[0] - 1) // 2
    steady = jnp.sum(block_mean * spectral_modes[0][None, :, :], axis=1)
    paired = spectral_modes[1:].reshape(harmonics, 2 * variables, spectral_modes.shape[2])
    paired = jnp.sum(block_wave * paired[:, None, :, :], axis=2)
    joined = jnp.concatenate(
        [steady[None], paired.reshape(2 * harmonics, variables, spectral_modes.shape[2])], axis=0
    )
    return jnp.einsum("kn,kvc->nvc", spectral, joined, precision=lax.Precision.HIGHEST)


def neighbor_sum(padded, offsets, coupling, reach_cells):
    cell_count = offsets.shape[1]
    cell_base = jnp.arange(cell_count, dtype=jnp.int32) + reach_cells
    accumulated = jnp.zeros((padded.shape[0], padded.shape[1], cell_count), jnp.float32)
    for neighbor in range(offsets.shape[0]):
        neighbor_vals = jnp.take(padded, cell_base + offsets[neighbor], axis=2)
        accumulated = accumulated + coupling[neighbor][None, :, :] * neighbor_vals
    return accumulated


def general(
    right_side, coupling, offsets, block_mean, block_wave, donor_cells, receiver_cells, inlet_gain
):
    space_rank = lax.axis_index("space")
    source_base = right_side[0]
    cell_count = source_base.shape[2]
    spectral = spectral_table(source_base.shape[0])
    first_cell = space_rank * cell_count
    mean_blocks = block_mean[0]
    wave_blocks = block_wave[0]

    def apply_inverse(values):
        return invert_blocks(values, mean_blocks, wave_blocks, spectral)

    donor_local = donor_cells[0] - first_cell
    donor_inside = ((donor_local >= 0) & (donor_local < cell_count)).astype(jnp.float32)
    donor_clip = jnp.clip(donor_local, 0, cell_count - 1)
    receiver_local = receiver_cells[0] - first_cell
    receiver_inside = ((receiver_local >= 0) & (receiver_local < cell_count)).astype(jnp.float32)
    receiver_clip = jnp.clip(receiver_local, 0, cell_count - 1)
    row_total = lax.axis_size("row")
    inlet_profile = jnp.zeros((NI, NV, NIF), jnp.float32)

    def row(_, carry):
        inlet_profile, _ = carry
        inflow = inlet_gain[0][None, :, :] * inlet_profile * receiver_inside[None, None, :]
        source = source_base - jnp.zeros_like(source_base).at[:, :, receiver_clip].add(inflow)

        def sweep(_, state):
            padded = with_halo(state, (("space", 2),), HALO)
            coupled = neighbor_sum(padded, offsets[0], coupling[0], HALO)
            return apply_inverse(source - coupled)

        state_field = lax.fori_loop(0, SWEEPS, sweep, apply_inverse(source))
        outgoing = jnp.take(state_field, donor_clip, axis=2) * donor_inside[None, None, :]
        return from_behind(sum_over(outgoing, "space"), "row", 1), state_field

    return lax.fori_loop(0, row_total, row, (inlet_profile, source_base))[1][None]


def on_device(*args):
    modes, flag = fast(*args)
    return lax.cond(flag[0, 0] > 0, lambda: general(*args), lambda: finish(modes))


def solution(mesh):
    return jax.shard_map(
        on_device,
        mesh=mesh,
        in_specs=(
            P("row", None, None, "space"),
            P("row", None, None, "space"),
            P("row", None, "space"),
            P("row", None, None, "space"),
            P("row", None, None, None, "space"),
            P("row", None),
            P("row", None),
            P("row", None, None),
        ),
        out_specs=P("row", None, None, "space"),
        check_vma=False,
    )
```

```python
import functools
import math

import jax
import jax.numpy as jnp
import numpy as np
from jax import lax
from jax.experimental import pallas as pl
from jax.experimental.pallas import tpu as pltpu
from jax.sharding import PartitionSpec as P

NI = 9
NV = 5
NF = NI * NV
NOFF = 6
HALO = 16
SWEEPS = 2
NIF = 1024
ROWS = 4
NS = 64
GROUP = 8
FAR = (4, 3, 5, 2, 6, 1, 7, 0)
OWN = 512
EDGE = 32
CAP = 6
MESH = pl.DeviceIdType.MESH

HALO_ROWS = 136
AT_BASE = 104
AT_SOURCE = 512


def field_row(f):
    return (f if f < 25 else f + 7) * 8


def spectral_numbers():
    n = np.arange(NI, dtype=np.float64)
    table = [np.full(NI, 1.0 / math.sqrt(NI))]
    for k in range(1, (NI - 1) // 2 + 1):
        table.append(math.sqrt(2.0 / NI) * np.cos(2.0 * math.pi * k * n / NI))
        table.append(math.sqrt(2.0 / NI) * np.sin(2.0 * math.pi * k * n / NI))
    return np.stack(table).astype(np.float32)


def own_tile(ref, row, n, m):
    lane = lax.broadcasted_iota(jnp.int32, (n, 128), 1)
    even = ref[pl.ds(row + 2 * m, n, stride=8), :]
    odd = ref[pl.ds(row + 2 * m + 1, n, stride=8), :]
    return jnp.where(lane < 64, pltpu.roll(even, 96, 1), pltpu.roll(odd, 32, 1))


def finish_kernel(x_w, out_ref, y_w):
    lane4 = lax.broadcasted_iota(jnp.int32, (4, 128), 1)
    table = spectral_numbers()
    for v in range(NV):
        parts = [x_w[pl.ds(field_row(m * NV + v), 8), :] for m in range(NI)]
        for n in range(NI):
            total = float(table[0, n]) * parts[0]
            for m in range(1, NI):
                total = total + float(table[m, n]) * parts[m]
            y_w[pl.ds((n * NV + v) * 8, 8), :] = total

    def out_rows(i, c):
        even = y_w[pl.ds(i * 8, 4, stride=2), :]
        odd = y_w[pl.ds(i * 8 + 1, 4, stride=2), :]
        out_ref[i] = jnp.where(lane4 < 64, pltpu.roll(even, 96, 1), pltpu.roll(odd, 32, 1))
        return c

    lax.fori_loop(0, NF, out_rows, 0, unroll=9)


def finish(modes):
    return pl.pallas_call(
        finish_kernel,
        out_shape=jax.ShapeDtypeStruct((NF, 4, 128), jnp.float32),
        scratch_shapes=[pltpu.VMEM((NF * 8 + 8, 128), jnp.float32)],
        cost_estimate=pl.CostEstimate(flops=2 * NI * NF * 1024, bytes_accessed=500000, transcendentals=0),
    )(modes).reshape(1, NI, NV, OWN)


def kernel(
    rhs_h, cpl_h, off_h, bm_h, bw_h, don_h, rec_h, gain_h,
    x_w, flag_ref,
    rhs_v, cpl_v, off_v, bm_v, bw_v, gain_v, idx_v,
    wave_w, base_w, edge_s, lane_w,
    send_left, send_right, from_left, from_right,
    code_s, sel_s, xr_s, wr_s, gpk_s, msg_s, got_s,
    in_sem, idx_send, idx_recv, edge_send, edge_recv, msg_send, msg_recv, ready,
):
    r = lax.axis_index("row")
    s = lax.axis_index("space")

    z, p = s // GROUP, s % GROUP

    bar = pltpu.get_barrier_semaphore()

    def greet(row, t):
        pl.semaphore_signal(bar, inc=1, device_id=(row, t), device_id_type=MESH)

    @pl.when(r < ROWS - 1)
    def _():
        for j in range(GROUP):
            greet(r + 1, z * GROUP + j)

    @pl.when(r > 0)
    def _():
        for j in range(GROUP):
            greet(r - 1, z * GROUP + j)

    for d in FAR[:-1]:
        greet(r, lax.rem(z + d, GROUP) * GROUP + p)

    @pl.when(s > 0)
    def _():
        greet(r, s - 1)

    @pl.when(s < NS - 1)
    def _():
        greet(r, s + 1)

    for row in range(ROWS):
        @pl.when((row > r + 1) | (row < r - 1))
        def _():
            greet(row, s)

    loads = [
        pltpu.make_async_copy(bw_h, bw_v, in_sem.at[0]),
        pltpu.make_async_copy(bm_h, bm_v, in_sem.at[1]),
        pltpu.make_async_copy(cpl_h, cpl_v, in_sem.at[2]),
        pltpu.make_async_copy(rhs_h, rhs_v, in_sem.at[3]),
        pltpu.make_async_copy(off_h, off_v, in_sem.at[4]),
        pltpu.make_async_copy(gain_h, gain_v, in_sem.at[5]),
        pltpu.make_async_copy(don_h, idx_v.at[r, 0], in_sem.at[6]),
        pltpu.make_async_copy(rec_h, idx_v.at[r, 1], in_sem.at[7]),
    ]
    for c in loads:
        c.start()

    lane8 = lax.broadcasted_iota(jnp.int32, (8, 128), 1)

    def to_windows(tiles, dst, row):
        n = tiles[0].shape[0]
        lane = lane8[:n]
        up = [pltpu.roll(t, 32, 1) for t in tiles]
        down = [pltpu.roll(t, 96, 1) for t in tiles]
        for m in range(4):
            even = up[m] if m == 0 else jnp.where(lane < 32, up[m - 1], up[m])
            odd = down[m] if m == 3 else jnp.where(lane < 96, down[m], down[m + 1])
            dst[pl.ds(row + 2 * m, n, stride=8), :] = even
            dst[pl.ds(row + 2 * m + 1, n, stride=8), :] = odd

    def pack(firsts, lasts, row):
        n = firsts[0].shape[0]
        lane = lane8[:n]
        left = firsts[0]
        right = pltpu.roll(lasts[0], 32, 1)
        for e in range(1, len(firsts)):
            left = jnp.where(lane >= 32 * e, pltpu.roll(firsts[e], 32 * e, 1), left)
            moved = lasts[e] if e == 3 else pltpu.roll(lasts[e], (32 * e + 32) % 128, 1)
            right = jnp.where(lane >= 32 * e, moved, right)
        send_left[pl.ds(row, n), :] = left
        send_right[pl.ds(row, n), :] = right

    loads[0].wait()

    def wave_tile(u, m):
        return jnp.concatenate([bw_v[2 * u + i, :, pl.ds(128 * m, 128)] for i in range(2)], axis=0)

    def wave_pack(p, c):
        pack([wave_tile(4 * p + e, 0) for e in range(4)], [wave_tile(4 * p + e, 3) for e in range(4)], 8 * p)
        return c

    lax.fori_loop(0, 12, wave_pack, 0, unroll=4)
    pack([wave_tile(48 + e, 0) for e in range(2)], [wave_tile(48 + e, 3) for e in range(2)], 96)

    for c in loads[1:5]:
        c.wait()
    table = spectral_numbers()
    for v in range(NV):
        parts = [rhs_v[n * NV + v] for n in range(NI)]
        for m in range(NI):
            total = float(table[m, 0]) * parts[0]
            for n in range(1, NI):
                total = total + float(table[m, n]) * parts[n]
            rhs_v[m * NV + v] = total

    base_parts = (
        (bm_v, 0, 0, 25), (cpl_v, 0, 25, 30), (off_v, 0, 55, 6), (rhs_v, 0, 64, 25), (rhs_v, 25, 96, 20))
    for ref, skip, first, count in base_parts:
        for i in range(count):
            tile = ref[skip + i].astype(jnp.float32)
            edge_s[0, pl.ds(first + i, 1), :] = tile[0:1]
            edge_s[1, pl.ds(first + i, 1), :] = tile[3:4]
    for first, count in ((61, 3), (89, 7), (116, 12)):
        edge_s[:, pl.ds(first, count), :] = jnp.zeros((2, count, 128), jnp.float32)
        base_w[pl.ds(first * 8, count * 8), :] = jnp.zeros((count * 8, 128), jnp.float32)
    for q in range(4):
        pack(
            [edge_s[0, pl.ds(32 * e + 8 * q, 8), :] for e in range(4)],
            [edge_s[1, pl.ds(32 * e + 8 * q, 8), :] for e in range(4)], AT_BASE + 8 * q)
    for c in loads[5:]:
        c.wait()
    x_w[pl.ds(200, 56), :] = jnp.zeros((56, 128), jnp.float32)
    x_w[pl.ds(416, 104), :] = jnp.zeros((104, 128), jnp.float32)

    @pl.when(s == 0)
    def _():
        from_left[...] = jnp.zeros(from_left.shape, jnp.float32)

    @pl.when(s == NS - 1)
    def _():
        from_right[...] = jnp.zeros(from_right.shape, jnp.float32)

    def one_if(condition):
        return jnp.where(condition, 1, 0)

    here = GROUP * (one_if(r > 0) + one_if(r < ROWS - 1)) + GROUP - 1
    here = here + one_if(s > 0) + one_if(s < NS - 1)
    here = here + 1 + one_if(r == 0) + one_if(r == ROWS - 1)
    pl.semaphore_wait(bar, here)

    @pl.when(r > 0)
    def _():
        for j in range(GROUP):
            at = (r - 1, z * GROUP + j)
            pl.semaphore_signal(ready, inc=1, device_id=at, device_id_type=MESH)

    def index_copy(d, part, sem):
        at = idx_v.at[r] if part is None else idx_v.at[r, part]
        return pltpu.make_async_remote_copy(
            at, at, idx_send.at[sem], idx_recv.at[sem],
            device_id=(lax.rem(r + d, ROWS), s), device_id_type=MESH)

    index_copies = [index_copy(ROWS - 1, 1, 0), index_copy(1, None, 1), index_copy(2, None, 2), index_copy(ROWS - 1, 0, 3)]
    index_copies[0].start()
    right = pltpu.make_async_remote_copy(
        send_right, from_left, edge_send.at[0], edge_recv.at[0],
        device_id=(r, lax.rem(s + 1, NS)), device_id_type=MESH)
    left = pltpu.make_async_remote_copy(
        send_left, from_right, edge_send.at[1], edge_recv.at[1],
        device_id=(r, lax.rem(s + NS - 1, NS)), device_id_type=MESH)

    @pl.when(s < NS - 1)
    def _():
        right.start()

    @pl.when(s > 0)
    def _():
        left.start()

    for c in index_copies[1:]:
        c.start()

    def wave_windows(u, c):
        to_windows([wave_tile(u, m) for m in range(4)], wave_w, u * 64)
        return c

    lax.fori_loop(0, 50, wave_windows, 0, unroll=10)
    lane4 = lane8[:4]
    for ref, skip, first, count in base_parts:
        def base_rows(i, c, ref=ref, skip=skip, first=first):
            tile = ref[skip + i].astype(jnp.float32)
            up = pltpu.roll(tile, 32, 1)
            down = pltpu.roll(tile, 96, 1)
            at = (first + i) * 8
            base_w[pl.ds(at, 4, stride=2), :] = jnp.where(lane4 < 32, pltpu.roll(up, 1, 0), up)
            base_w[pl.ds(at + 1, 4, stride=2), :] = jnp.where(lane4 < 96, down, pltpu.roll(down, 3, 0))
            return c
        lax.fori_loop(0, count, base_rows, 0, unroll=5 if count % 5 == 0 else 6)

    dev64 = lax.broadcasted_iota(jnp.int32, (NS, 1), 0)
    tri = (lax.broadcasted_iota(jnp.int32, (128, 128), 0) <= lax.broadcasted_iota(jnp.int32, (128, 128), 1))
    tri = tri.astype(jnp.float32).astype(jnp.bfloat16)

    def order(mask):
        before = jnp.zeros((NS, 1), jnp.float32)
        for b in range(NIF // 128):
            m = mask[:, 128 * b:128 * b + 128]
            upto = jnp.dot(m.astype(jnp.bfloat16), tri, preferred_element_type=jnp.float32)
            code_s[:, pl.ds(128 * b, 128)] = jnp.where(m > 0.5, before + upto - 1.0, -1.0)
            before = before + jnp.sum(m, axis=1, keepdims=True)

    def pick(k, value):
        return jnp.sum(jnp.where(code_s[...] == float(k), value, 0.0), axis=1, keepdims=True)

    def in_block(cells, device):
        low = device * OWN
        return (cells >= low) & (cells < low + OWN)

    def in_windows(cells, device):
        low = device * OWN - EDGE
        return (cells >= low) & (cells < low + OWN + 2 * EDGE)

    @pl.when(r < ROWS - 1)
    def _():
        index_copies[0].wait_recv()
        donor = idx_v[r, 0]
        receiver = idx_v[r + 1, 1]
        order((in_block(donor, s) & in_windows(receiver, dev64)).astype(jnp.float32))
        place = (donor - s * OWN + 1).astype(jnp.float32)
        cell = lax.broadcasted_iota(jnp.int32, (NS, OWN), 1).astype(jnp.float32) + 1.0
        for k in range(CAP):
            hit = (pick(k, place) == cell).astype(jnp.float32).astype(jnp.bfloat16)
            sel_s[pl.ds(k * NS, NS), :] = hit

    @pl.when(r > 0)
    def _():
        index_copies[1].wait_recv()
        donor = idx_v[r - 1, 0]
        receiver = idx_v[r, 1]
        order((in_block(donor, dev64) & in_windows(receiver, s)).astype(jnp.float32))
        place = (receiver - s * OWN + EDGE + 1).astype(jnp.float32)
        position = lax.broadcasted_iota(jnp.int32, (NS, 1024), 1)
        cell = ((position // 128) * 64 + position % 128 + 1).astype(jnp.float32)
        lane = lax.broadcasted_iota(jnp.int32, (1, 128), 1)
        field = lane % 32
        for k in range(CAP):
            hit = (pick(k, place) == cell).astype(jnp.float32).astype(jnp.bfloat16)
            wr_s[pl.ds(k * NS, NS), :] = hit
        for k in range(2):
            rows = jnp.zeros((NS, 128), jnp.float32)
            for v in range(NV):
                for g in range(CAP // 2):
                    mine = (field % NV == v) & (field < 25) & (lane // 32 == g)
                    rows = rows + jnp.where(mine, pick(2 * g + k, gain_v[v]), 0.0)
            gpk_s[pl.ds(k * NS, NS), :] = rows

    @pl.when(s > 0)
    def _():
        right.wait_recv()

    @pl.when(s < NS - 1)
    def _():
        left.wait_recv()

    def merge(dst, row, n, src_row, e):
        lane = lane8[:n]
        low = from_left[pl.ds(src_row, n), :]
        low = low if e == 0 else pltpu.roll(low, 128 - 32 * e, 1)
        high = from_right[pl.ds(src_row, n), :]
        high = high if e == 3 else pltpu.roll(high, 96 - 32 * e, 1)
        at = pl.ds(row, n, stride=8)
        dst[at, :] = jnp.where(lane < 32, low, dst[at, :])
        at = pl.ds(row + 7, n, stride=8)
        dst[at, :] = jnp.where(lane >= 96, high, dst[at, :])

    def wave_edges(p, c):
        for e in range(4):
            merge(wave_w, (4 * p + e) * 64, 8, 8 * p, e)
        return c

    lax.fori_loop(0, 12, wave_edges, 0, unroll=12)
    for e in range(2):
        merge(wave_w, (48 + e) * 64, 8, 96, e)
    for e in range(4):
        for q in range(4 if e < 3 else 3):
            merge(base_w, (32 * e + 8 * q) * 8, 8, AT_BASE + 8 * q, e)

    for j in range(NOFF):
        at = lane8 + base_w[pl.ds((55 + j) * 8, 8), :].astype(jnp.int32)
        lane_w[j] = jnp.clip(at, 0, 127)

    def inflow(h):
        pltpu.make_async_remote_copy(
            msg_s.at[h], got_s.at[h], msg_send.at[h], msg_recv.at[h],
            device_id=(r - 1, s), device_id_type=MESH).wait_recv()
        rows = jnp.concatenate([got_s[h, :, k, :] for k in range(2)], axis=0) * gpk_s[...]
        turned = rows.T
        both = jnp.concatenate([turned[32 * g:32 * g + 32] for g in range(CAP // 2)], axis=1)
        high = both.astype(jnp.bfloat16)
        low = (both - high.astype(jnp.float32)).astype(jnp.bfloat16)
        added = jnp.dot(jnp.concatenate([high, low], axis=0), wr_s[...], preferred_element_type=jnp.float32)
        added = added[:32] + added[32:]
        for a in range(4 - h):
            for j in range(8):
                at = pl.ds(AT_SOURCE + h * 256 + a * 64 + j, 8, stride=8)
                base_w[at, :] = base_w[at, :] - added[8 * a:8 * a + 8, 128 * j:128 * j + 128]

    def relax(row, count, entry):
        source = [base_w[pl.ds(AT_SOURCE + row + f * 8, 8), :] for f in range(count)]

        def solve(values):
            result = []
            for f in range(count):
                total = None
                for g in range(count):
                    term = entry(f, g) * values[g]
                    total = term if total is None else total + term
                result.append(total)
            return result

        x = solve(source)
        for _ in range(SWEEPS):
            rest = list(source)
            for j in range(NOFF):
                at = lane_w[j]
                for f in range(count):
                    moved = jnp.take_along_axis(x[f], at, axis=1, mode="promise_in_bounds")
                    rest[f] = rest[f] - base_w[pl.ds((25 + j * NV + f % NV) * 8, 8), :] * moved
            x = solve(rest)
        for f in range(count):
            x_w[pl.ds(row + f * 8, 8), :] = x[f]

    def harmonic(k, c):
        row = 40 + 80 * k if k < 2 else 256 + 80 * (k - 2)
        relax(row, 10, lambda f, g: wave_w[pl.ds((f * 10 + g) * 32 + k * 8, 8), :])
        return c

    def relax_half(h):
        if h == 0:
            relax(0, NV, lambda f, g: base_w[pl.ds((f * NV + g) * 8, 8), :])
        for k in (2 * h, 2 * h + 1):
            harmonic(k, 0)

    def donate(h):
        for a in range(2):
            for m in range(4):
                tile = jnp.concatenate(
                    [own_tile(x_w, h * 256 + (2 * a + i) * 64, 8, m) for i in range(2)], axis=0)
                high = tile.astype(jnp.bfloat16)
                low = (tile - high.astype(jnp.float32)).astype(jnp.bfloat16)
                xr_s[pl.ds(16 * a, 16), pl.ds(128 * m, 128)] = high
                xr_s[pl.ds(32 + 16 * a, 16), pl.ds(128 * m, 128)] = low
        values = lax.dot_general(
            xr_s[...], sel_s[...], (((1,), (1,)), ((), ())), preferred_element_type=jnp.float32)
        values = values[:32] + values[32:]
        groups = [values[:, 128 * g:128 * g + 128] for g in range(CAP // 2)]
        groups += [jnp.zeros((32, 128), jnp.float32)] * (4 - CAP // 2)
        rows = jnp.concatenate(groups, axis=0).T
        for k in range(2):
            msg_s[h, :, k, :] = rows[k * NS:(k + 1) * NS]
        if h == 0:
            pl.semaphore_wait(ready, GROUP)

        for d in FAR:
            plane = lax.rem(z + d, GROUP) * GROUP
            for j in range(GROUP):
                t = plane + j
                pltpu.make_async_remote_copy(
                    msg_s.at[h, t], got_s.at[h, s], msg_send.at[h], msg_recv.at[h],
                    device_id=(r + 1, t), device_id_type=MESH).start()

    def check():
        @pl.when(r == ROWS - 1)
        def _():
            index_copies[0].wait_recv()

        @pl.when(r == 0)
        def _():
            index_copies[1].wait_recv()

        index_copies[2].wait_recv()
        index_copies[3].wait_recv()
        most = jnp.zeros((NS, NS), jnp.float32)
        for row in range(ROWS - 1):
            gives = in_block(idx_v[row, 0], dev64).astype(jnp.float32).astype(jnp.bfloat16)
            takes = in_windows(idx_v[row + 1, 1], dev64).astype(jnp.float32).astype(jnp.bfloat16)
            count = lax.dot_general(gives, takes, (((1,), (1,)), ((), ())), preferred_element_type=jnp.float32)
            most = jnp.maximum(most, count)
        flag_ref[0, 0] = jnp.where(jnp.max(most) > CAP + 0.5, 1, 0)

    @pl.when(r > 0)
    def _():
        check()

    for h in range(2):
        @pl.when(r > 0)
        def _():
            inflow(h)

        relax_half(h)

        @pl.when(r < ROWS - 1)
        def _():
            donate(h)

    @pl.when(r == 0)
    def _():
        check()

    for c in index_copies:
        c.wait_send()

    @pl.when(s < NS - 1)
    def _():
        right.wait_send()

    @pl.when(s > 0)
    def _():
        left.wait_send()

    @pl.when(r < ROWS - 1)
    def _():
        for h in range(2):
            pltpu.make_async_remote_copy(
                msg_s.at[h], got_s.at[h], msg_send.at[h], msg_recv.at[h],
                device_id=(r + 1, s), device_id_type=MESH).wait_send()


def fast(rhs, cpl, off, bm, bw, don, rec, gain):
    bw = jnp.transpose(bw, (0, 2, 3, 1, 4)).reshape(100, 4, OWN)
    rhs, cpl, off, bm = (a.reshape(-1, 4, 128) for a in (rhs, cpl, off, bm))
    gain = gain.reshape(NV, 1, NIF)
    any_space = pl.BlockSpec(memory_space=pl.ANY)
    vmem = pl.BlockSpec(memory_space=pltpu.VMEM)
    f32, i32, bf16 = jnp.float32, jnp.int32, jnp.bfloat16
    return pl.pallas_call(
        kernel,
        out_shape=(jax.ShapeDtypeStruct((520, 128), f32), jax.ShapeDtypeStruct((1, 1), i32)),
        in_specs=[any_space] * 8,
        out_specs=(vmem, pl.BlockSpec(memory_space=pltpu.SMEM)),
        scratch_shapes=[
            pltpu.VMEM((NF, 4, 128), f32),
            pltpu.VMEM((NOFF * NV, 4, 128), f32),
            pltpu.VMEM((NOFF, 4, 128), i32),
            pltpu.VMEM((NV * NV, 4, 128), f32),
            pltpu.VMEM((100, 4, OWN), f32),
            pltpu.VMEM((NV, 1, NIF), f32),
            pltpu.VMEM((ROWS, 2, 1, NIF), i32),
            pltpu.VMEM((3208, 128), f32),
            pltpu.VMEM((1024, 128), f32),
            pltpu.VMEM((2, 128, 128), f32),
            pltpu.VMEM((NOFF, 8, 128), i32),
            pltpu.VMEM((HALO_ROWS, 128), f32),
            pltpu.VMEM((HALO_ROWS, 128), f32),
            pltpu.VMEM((HALO_ROWS, 128), f32),
            pltpu.VMEM((HALO_ROWS, 128), f32),
            pltpu.VMEM((NS, NIF), f32),
            pltpu.VMEM((CAP * NS, OWN), bf16),
            pltpu.VMEM((64, OWN), bf16),
            pltpu.VMEM((CAP * NS, 1024), bf16),
            pltpu.VMEM((2 * NS, 128), f32),
            pltpu.VMEM((2, NS, 2, 128), f32),
            pltpu.VMEM((2, NS, 2, 128), f32),
            pltpu.SemaphoreType.DMA((8,)),
            pltpu.SemaphoreType.DMA((ROWS,)),
            pltpu.SemaphoreType.DMA((ROWS,)),
            pltpu.SemaphoreType.DMA((2,)),
            pltpu.SemaphoreType.DMA((2,)),
            pltpu.SemaphoreType.DMA((2,)),
            pltpu.SemaphoreType.DMA((2,)),
            pltpu.SemaphoreType.REGULAR,
        ],
        compiler_params=pltpu.CompilerParams(
            collective_id=0, has_side_effects=True, vmem_limit_bytes=40 * 1024 * 1024),
    )(rhs, cpl, off, bm, bw, don, rec, gain)


def with_halo(block, sides, width):
    for axis, dim in sides:
        count = lax.axis_size(axis)
        forward = [(i, i + 1) for i in range(count - 1)]
        backward = [(target, source) for source, target in forward]
        low = lax.ppermute(
            lax.slice_in_dim(block, block.shape[dim] - width, None, axis=dim), axis, forward
        )
        high = lax.ppermute(lax.slice_in_dim(block, 0, width, axis=dim), axis, backward)
        block = jnp.concatenate([low, block, high], axis=dim)
    return block


def from_behind(value, axis, steps):
    count = lax.axis_size(axis)
    first, last = (max(0, -steps), min(count, count - steps))
    return lax.ppermute(value, axis, [(source, source + steps) for source in range(first, last)])


def sum_over(value, axis):
    count = lax.axis_size(axis)
    step = 1
    while step < count:
        value = value + lax.ppermute(value, axis, [(i, i ^ step) for i in range(count)])
        step *= 2
    return value


def spectral_table(instances):
    position = jnp.arange(instances).astype(jnp.float32)
    harmonic = jnp.arange(1, (instances - 1) // 2 + 1).astype(jnp.float32)
    phase_angle = 2.0 * math.pi / instances * harmonic[:, None] * position[None, :]
    weight = math.sqrt(2.0 / instances)
    wave_rows = jnp.stack(
        [weight * jnp.cos(phase_angle), weight * jnp.sin(phase_angle)], axis=1
    ).reshape(-1, instances)
    mean_row = jnp.full((1, instances), 1.0 / math.sqrt(instances), jnp.float32)
    return jnp.concatenate([mean_row, wave_rows], axis=0)


def invert_blocks(values, block_mean, block_wave, spectral):
    spectral_modes = jnp.einsum("kn,nvc->kvc", spectral, values, precision=lax.Precision.HIGHEST)
    variables = spectral_modes.shape[1]
    harmonics = (spectral_modes.shape[0] - 1) // 2
    steady = jnp.sum(block_mean * spectral_modes[0][None, :, :], axis=1)
    paired = spectral_modes[1:].reshape(harmonics, 2 * variables, spectral_modes.shape[2])
    paired = jnp.sum(block_wave * paired[:, None, :, :], axis=2)
    joined = jnp.concatenate(
        [steady[None], paired.reshape(2 * harmonics, variables, spectral_modes.shape[2])], axis=0
    )
    return jnp.einsum("kn,kvc->nvc", spectral, joined, precision=lax.Precision.HIGHEST)


def neighbor_sum(padded, offsets, coupling, reach_cells):
    cell_count = offsets.shape[1]
    cell_base = jnp.arange(cell_count, dtype=jnp.int32) + reach_cells
    accumulated = jnp.zeros((padded.shape[0], padded.shape[1], cell_count), jnp.float32)
    for neighbor in range(offsets.shape[0]):
        neighbor_vals = jnp.take(padded, cell_base + offsets[neighbor], axis=2)
        accumulated = accumulated + coupling[neighbor][None, :, :] * neighbor_vals
    return accumulated


def general(
    right_side, coupling, offsets, block_mean, block_wave, donor_cells, receiver_cells, inlet_gain
):
    space_rank = lax.axis_index("space")
    source_base = right_side[0]
    cell_count = source_base.shape[2]
    spectral = spectral_table(source_base.shape[0])
    first_cell = space_rank * cell_count
    mean_blocks = block_mean[0]
    wave_blocks = block_wave[0]

    def apply_inverse(values):
        return invert_blocks(values, mean_blocks, wave_blocks, spectral)

    donor_local = donor_cells[0] - first_cell
    donor_inside = ((donor_local >= 0) & (donor_local < cell_count)).astype(jnp.float32)
    donor_clip = jnp.clip(donor_local, 0, cell_count - 1)
    receiver_local = receiver_cells[0] - first_cell
    receiver_inside = ((receiver_local >= 0) & (receiver_local < cell_count)).astype(jnp.float32)
    receiver_clip = jnp.clip(receiver_local, 0, cell_count - 1)
    row_total = lax.axis_size("row")
    inlet_profile = jnp.zeros((NI, NV, NIF), jnp.float32)

    def row(_, carry):
        inlet_profile, _ = carry
        inflow = inlet_gain[0][None, :, :] * inlet_profile * receiver_inside[None, None, :]
        source = source_base - jnp.zeros_like(source_base).at[:, :, receiver_clip].add(inflow)

        def sweep(_, state):
            padded = with_halo(state, (("space", 2),), HALO)
            coupled = neighbor_sum(padded, offsets[0], coupling[0], HALO)
            return apply_inverse(source - coupled)

        state_field = lax.fori_loop(0, SWEEPS, sweep, apply_inverse(source))
        outgoing = jnp.take(state_field, donor_clip, axis=2) * donor_inside[None, None, :]
        return from_behind(sum_over(outgoing, "space"), "row", 1), state_field

    return lax.fori_loop(0, row_total, row, (inlet_profile, source_base))[1][None]


def on_device(*args):
    modes, flag = fast(*args)
    return lax.cond(flag[0, 0] > 0, lambda: general(*args), lambda: finish(modes))


def solution(mesh):
    return jax.shard_map(
        on_device,
        mesh=mesh,
        in_specs=(
            P("row", None, None, "space"),
            P("row", None, None, "space"),
            P("row", None, "space"),
            P("row", None, None, "space"),
            P("row", None, None, None, "space"),
            P("row", None),
            P("row", None),
            P("row", None, None),
        ),
        out_specs=P("row", None, None, "space"),
        check_vma=False,
    )
```
